32 devices in a mesh: view: 16 (over z, x, core), tok: 2 (over y).
Axes of the slice: x: 2, y: 2, z: 4, core: 2. Of those that a mesh axis runs over, the one named last changes fastest.
Arguments:
- queries: bfloat16 [48, 98, 1024], P('view', 'tok'), may hold values from -6 to 6
- keys: bfloat16 [48, 98, 1024], P('view', 'tok'), may hold values from -6 to 6
- values: bfloat16 [48, 98, 1024], P('view', 'tok'), may hold values from -6 to 6
- grad_out: bfloat16 [48, 98, 1024], P('view', 'tok'), may hold values from -6 to 6
Outputs:
- attended: bfloat16 [48, 98, 1024], P('view', 'tok')
- query_grad: bfloat16 [48, 98, 1024], P('view', 'tok')
- key_grad: bfloat16 [48, 98, 1024], P('view', 'tok')
- value_grad: bfloat16 [48, 98, 1024], P('view', 'tok')
The draws below stay inside these ranges and needn't reach their ends.
All inputs are finite; a program needn't handle non-finite values.
Results may differ from the reference program's by a relative error of at most 0.03.
Values may be sent and summed in bfloat16 or wider, within the bound.
A program may use at most 128 MiB of HBM per device.

```python
import math
import jax
import jax.numpy as jnp
from jax import lax

D = 1024
HEADS = 16
HEAD_DIM = 64
TOK_SHARD = 49
VIEWS = 48
VTOK = 98
N_TOK = 2


def draw_queries(key, part):
    key = jax.random.fold_in(key, 11)
    base = jnp.clip(jax.random.normal(key, (VIEWS, VTOK, D), jnp.float32), -6.0, 6.0)
    return base.astype(jnp.bfloat16)


def draw_keys(key, part):
    key = jax.random.fold_in(key, 23)
    base = jnp.clip(jax.random.normal(key, (VIEWS, VTOK, D), jnp.float32), -6.0, 6.0)
    return base.astype(jnp.bfloat16)


def block_levels(rng, dims, cuts, least, top_value):
    def one(axis_at, blocks):
        draws = jax.random.uniform(jax.random.fold_in(jax.random.fold_in(rng, 6), axis_at), (blocks,), jnp.float32, least / len(cuts), top_value / len(cuts))
        return jnp.repeat(jnp.exp(draws), dims[axis_at] // blocks).reshape((-1,) + (1,) * (len(dims) - axis_at - 1))

    gain = one(*cuts[0])
    for cut in cuts[1:]:
        gain = gain * one(*cut)
    return gain


def noise(key, shape, width, most, cuts=(), dtype=jnp.bfloat16):
    gain = block_levels(key, shape, cuts, -0.22, 0.18) if cuts else 1.0
    entries = jax.random.normal(key, shape, jnp.float32) * width * gain
    return jnp.minimum(jnp.maximum(entries, -most), most).astype(dtype)


def setup_inputs(seed: int = 0) -> dict:
    key_list = jax.random.split(jax.random.key(seed), 5)
    return {
        "queries": draw_queries(jax.random.fold_in(key_list[4], 71), 0),
        "keys": draw_keys(jax.random.fold_in(key_list[4], 71), 0),
        "values": noise(key_list[2], (VIEWS, VTOK, D), 1.0, 6.0, ((0, 16), (1, 2))),
        "grad_out": noise(key_list[3], (VIEWS, VTOK, D), 1.0, 6.0, ((0, 16), (1, 2))),
    }


def window_of(array, view_index):
    picks = (view_index + jnp.arange(-1, 2)) % VIEWS
    return jnp.take(array, picks.astype(jnp.int32), axis=0)

def reference(queries, keys, values, grad_out):
    score_scale = 1.0 / math.sqrt(HEAD_DIM)
    f32 = jnp.float32

    def forward_view(view_index):
        query_view = queries[view_index].reshape(VTOK, HEADS, HEAD_DIM).astype(f32)
        grad_view = grad_out[view_index].reshape(VTOK, HEADS, HEAD_DIM).astype(f32)
        key_window = window_of(keys, view_index).reshape(3 * VTOK, HEADS, HEAD_DIM).astype(f32)
        value_window = window_of(values, view_index).reshape(3 * VTOK, HEADS, HEAD_DIM).astype(f32)
        scores = jnp.einsum('qhd,khd->hqk', query_view, key_window) * score_scale
        row_max = lax.optimization_barrier(jnp.max(scores, axis=-1, keepdims=True))
        log_total = row_max[..., 0] + jnp.log(lax.optimization_barrier(jnp.sum(jnp.exp(scores - row_max), axis=-1)))
        probs = jnp.exp(scores - log_total[..., None])
        probs_bf = probs.astype(jnp.bfloat16)
        attended = jnp.einsum('hqk,khd->qhd', probs_bf.astype(f32), value_window).astype(jnp.bfloat16)
        row_delta = lax.optimization_barrier(jnp.sum(grad_view * attended.astype(f32), axis=-1)).T
        grad_probs = jnp.einsum('qhd,khd->hqk', grad_view, value_window)
        grad_scores = probs * (grad_probs - row_delta[..., None])
        grad_bf = grad_scores.astype(jnp.bfloat16)
        query_grad = (jnp.einsum('hqk,khd->qhd', grad_bf.astype(f32), key_window) * score_scale).astype(jnp.bfloat16)
        return (attended.reshape(VTOK, D), query_grad.reshape(VTOK, D), log_total, row_delta)
    attended, query_grad, log_totals, row_deltas = lax.map(forward_view, jnp.arange(VIEWS))

    def backward_keys(view_index):
        query_rows = window_of(queries, view_index).reshape(3 * VTOK, HEADS, HEAD_DIM).astype(f32)
        grad_rows = window_of(grad_out, view_index).reshape(3 * VTOK, HEADS, HEAD_DIM).astype(f32)
        total_rows = window_of(log_totals, view_index).transpose(1, 0, 2).reshape(HEADS, 3 * VTOK)
        delta_rows = window_of(row_deltas, view_index).transpose(1, 0, 2).reshape(HEADS, 3 * VTOK)
        key_rows = keys[view_index].reshape(VTOK, HEADS, HEAD_DIM).astype(f32)
        value_rows = values[view_index].reshape(VTOK, HEADS, HEAD_DIM).astype(f32)
        scores = jnp.einsum('qhd,khd->hqk', query_rows, key_rows) * score_scale
        probs = jnp.exp(scores - total_rows[..., None])
        probs_bf = probs.astype(jnp.bfloat16).astype(f32)
        grad_probs = jnp.einsum('qhd,khd->hqk', grad_rows, value_rows)
        grad_bf = (probs * (grad_probs - delta_rows[..., None])).astype(jnp.bfloat16).astype(f32)
        grad_split = grad_bf.reshape(HEADS, 3, N_TOK, TOK_SHARD, VTOK)
        probs_split = probs_bf.reshape(HEADS, 3, N_TOK, TOK_SHARD, VTOK)
        query_split = query_rows.reshape(3, N_TOK, TOK_SHARD, HEADS, HEAD_DIM)
        grad_out_split = grad_rows.reshape(3, N_TOK, TOK_SHARD, HEADS, HEAD_DIM)
        key_part = (jnp.einsum('hrgtk,rgthe->gkhe', grad_split, query_split) * score_scale).astype(jnp.bfloat16)
        value_part = jnp.einsum('hrgtk,rgthe->gkhe', probs_split, grad_out_split).astype(jnp.bfloat16)
        key_grad = lax.optimization_barrier(jnp.sum(key_part.astype(f32), axis=0)).astype(jnp.bfloat16)
        value_grad = lax.optimization_barrier(jnp.sum(value_part.astype(f32), axis=0)).astype(jnp.bfloat16)
        return (key_grad.reshape(VTOK, D), value_grad.reshape(VTOK, D))
    key_grad, value_grad = lax.map(backward_keys, jnp.arange(VIEWS))
    return (attended, query_grad, key_grad, value_grad)
```

```python
import functools
import math

import jax
import jax.numpy as jnp
from jax import lax
from jax.experimental import pallas as pl
from jax.experimental.pallas import tpu as pltpu
from jax.sharding import PartitionSpec as P

HEADS = 16
PAD = 64
NEG = -1e30
MESH = pl.DeviceIdType.MESH
F32 = jnp.float32
BF16 = jnp.bfloat16


def kernel(
    groups, parts, q_ref, k_ref, v_ref, g_ref, o_ref, dq_ref, dk_ref, dv_ref,
    qb, gb, kb, vb, ob, dqb, dkb, dvb, hk, hv, rk, rv,
    kp, vp, kt, vt, ak, av,
    in_send, in_recv, own_sem, halo_send, halo_recv, part_send, part_recv, out_send, out_recv,
):
    views, toks, width = q_ref.shape
    lanes = kp.shape[-1]
    half = lanes // 2
    share = width // parts
    chunks = share // lanes
    scale = 1.0 / math.sqrt(half)
    log2e = math.log2(math.e)
    whole8 = toks // 8 * 8
    up8 = (toks + 7) // 8 * 8
    me_v = lax.axis_index("view")
    me_t = lax.axis_index("tok")
    after = lax.rem(me_v + 1, groups)
    before = lax.rem(me_v + groups - 1, groups)
    peers = [lax.rem(me_t + s, parts) for s in range(parts)]

    barrier = pltpu.get_barrier_semaphore()
    for dev in [(before, me_t), (after, me_t)] + [(me_v, p) for p in peers[1:]]:
        pl.semaphore_signal(barrier, inc=1, device_id=dev, device_id_type=MESH)
    pl.semaphore_wait(barrier, parts + 1)

    def span(owner, c):
        return pl.ds(pl.multiple_of(owner * share + c * lanes, lanes), lanes)

    ins = (q_ref, g_ref, k_ref, v_ref)

    def landing(a, c, s):
        if a < 2:
            return (qb, gb)[a].at[c, s]
        return (kb, vb)[a - 2].at[c, s, pl.ds(1, views)]

    def in_copy(a, c, s):
        return pltpu.make_async_remote_copy(
            src_ref=ins[a].at[:, :, span(peers[s], c)],
            dst_ref=landing(a, c, parts - s),
            send_sem=in_send.at[c, s, a],
            recv_sem=in_recv.at[c, parts - s, a],
            device_id=(me_v, peers[s]),
            device_id_type=MESH,
        )

    def own_copy(a, c):
        return pltpu.make_async_copy(
            ins[a].at[:, :, span(me_t, c)], landing(a, c, 0), own_sem.at[c, a]
        )

    def halo_copy(a, c, s, way):
        buf = (kb, vb)[a]
        src, dst, dev = ((1, views + 1, before), (views, 0, after))[way]
        return pltpu.make_async_remote_copy(
            src_ref=buf.at[c, s, src],
            dst_ref=buf.at[c, s, dst],
            send_sem=halo_send.at[c, s, a, way],
            recv_sem=halo_recv.at[c, s, a, way],
            device_id=(dev, me_t),
            device_id_type=MESH,
        )

    def part_copy(a, c, way):
        return pltpu.make_async_remote_copy(
            src_ref=(hk, hv)[a].at[c, way],
            dst_ref=(rk, rv)[a].at[c, way],
            send_sem=part_send.at[c, a, way],
            recv_sem=part_recv.at[c, a, way],
            device_id=((before, after)[way], me_t),
            device_id_type=MESH,
        )

    outs = (o_ref, dq_ref, dk_ref, dv_ref)

    def out_copy(a, c, s):
        return pltpu.make_async_remote_copy(
            src_ref=(ob, dqb, dkb, dvb)[a].at[c, s],
            dst_ref=outs[a].at[:, :, span(me_t, c)],
            send_sem=out_send.at[c, s, a],
            recv_sem=out_recv.at[c, parts - s, a],
            device_id=(me_v, peers[s]),
            device_id_type=MESH,
        )

    def out_arrival(a, c, s):
        return pltpu.make_async_remote_copy(
            src_ref=(ob, dqb, dkb, dvb)[a].at[c, s],
            dst_ref=outs[a].at[:, :, span(peers[s], c)],
            send_sem=out_send.at[c, s, a],
            recv_sem=out_recv.at[c, s, a],
            device_id=(me_v, peers[s]),
            device_id_type=MESH,
        )

    @pl.loop(0, chunks)
    def _(c):
        for s in range(1, parts):
            for a in (2, 3, 0, 1):
                in_copy(a, c, s).start()
        for a in (2, 3, 0, 1):
            own_copy(a, c).start()

    def pad(x):
        return jnp.concatenate([x, jnp.zeros((PAD - toks, lanes), x.dtype)], axis=0)

    def stage(c, w):
        for buf, rows, cols in ((kb, kp, kt), (vb, vp, vt)):
            block = jnp.concatenate([pad(buf[c, s, w]) for s in range(parts)], axis=0)
            rows[w] = block
            cols[w] = block.T

    lane = lax.broadcasted_iota(jnp.int32, (2 * PAD, lanes), 1)
    row_ok = lax.broadcasted_iota(jnp.int32, (up8 - whole8, 2 * lanes), 0) < toks - whole8
    blocks = 3 * parts

    def twin(x):
        zero = jnp.zeros_like(x)
        return jnp.concatenate([jnp.where(lane < half, x, zero), jnp.where(lane < half, zero, x)], 0)

    def full(x):
        filler = jnp.zeros((blocks, PAD - up8, 2 * lanes), F32)
        return jnp.concatenate([x, filler], axis=1).reshape(blocks * PAD, 2 * lanes).astype(BF16)

    def diagonal(x):
        return jnp.concatenate([x[:half, :lanes], x[half:, lanes:]], axis=0).T

    def dot(x, y):
        return jnp.dot(x, y, preferred_element_type=F32)

    def dot_t(x, y):
        return lax.dot_general(x, y, (((1,), (1,)), ((), ())), preferred_element_type=F32)

    def compute(c, v):
        key_rows = kp[v : v + 3].reshape(blocks * PAD, lanes)
        value_rows = vp[v : v + 3].reshape(blocks * PAD, lanes)
        key_cols = jnp.concatenate([kt[v + j] for j in range(3)], axis=1)
        value_cols = jnp.concatenate([vt[v + j] for j in range(3)], axis=1)
        for s in range(0, parts, 2):
            query = jnp.concatenate([pad(qb[c, s + i, v]) for i in range(2)], axis=0)
            grad = jnp.concatenate([pad(gb[c, s + i, v]) for i in range(2)], axis=0)
            query = twin(query * jnp.asarray(scale, BF16))
            grad = twin(grad)
            scores = dot_t(key_rows, query).reshape(blocks, PAD, 2 * lanes)
            tail = jnp.where(row_ok[None], scores[:, whole8:up8], NEG)
            scores = jnp.concatenate([scores[:, :whole8], tail], axis=1)
            top = jnp.max(scores, axis=(0, 1), keepdims=True)
            probs = jnp.exp2((scores - top) * log2e)
            probs = probs * (1.0 / jnp.sum(probs, axis=(0, 1), keepdims=True))
            grad_probs = dot_t(value_rows, grad).reshape(blocks, PAD, 2 * lanes)[:, :up8]
            weighted = probs * grad_probs
            delta = jnp.sum(weighted, axis=(0, 1), keepdims=True)
            probs_bf = full(probs)
            grad_bf = full(weighted - probs * delta)
            key_term = dot(grad_bf, query).reshape(3, parts * PAD, lanes)
            value_term = dot(probs_bf, grad).reshape(3, parts * PAD, lanes)
            ak[v : v + 3] += key_term
            av[v : v + 3] += value_term
            attended = diagonal(dot(value_cols, probs_bf)).astype(BF16)
            query_grad = (diagonal(dot(key_cols, grad_bf)) * scale).astype(BF16)
            for i in range(2):
                rows = slice(i * PAD, i * PAD + toks)
                if s + i == 0:
                    o_ref[v, :, span(me_t, c)] = attended[rows]
                    dq_ref[v, :, span(me_t, c)] = query_grad[rows]
                else:
                    ob[c, s + i, v] = attended[rows]
                    dqb[c, s + i, v] = query_grad[rows]

    def finish(c, sums_k, sums_v):
        for a, (sums, buf, ref, got) in enumerate(
            ((sums_k, dkb, dk_ref, rk), (sums_v, dvb, dv_ref, rv))
        ):
            part_copy(a, c, 0).wait_recv()
            part_copy(a, c, 1).wait_recv()
            for s in range(parts):
                for v in range(views):
                    total = sums[v + 1, s * PAD : s * PAD + toks]
                    if v == 0:
                        total = total + got[c, 1, s].astype(F32)
                    if v == views - 1:
                        total = total + got[c, 0, s].astype(F32)
                    if s == 0:
                        ref[v, :, span(me_t, c)] = total.astype(BF16)
                    else:
                        buf[c, s, v] = total.astype(BF16)
            for s in range(1, parts):
                out_copy(2 + a, c, s).start()

    @pl.loop(0, chunks)
    def _(c):
        for a in (2, 3):
            own_copy(a, c).wait()
        for a in range(2):
            for way in range(2):
                halo_copy(a, c, 0, way).start()
        for s in range(1, parts):
            for a in (2, 3):
                in_copy(a, c, parts - s).wait_recv()
            for a in range(2):
                for way in range(2):
                    halo_copy(a, c, s, way).start()
        for w in range(1, views + 1):
            stage(c, w)
        ak[...] = jnp.zeros_like(ak)
        av[...] = jnp.zeros_like(av)
        for a in (0, 1):
            own_copy(a, c).wait()
            for s in range(1, parts):
                in_copy(a, c, parts - s).wait_recv()
        for v in range(1, views - 1):
            compute(c, v)
        for s in range(parts):
            for a in range(2):
                for way in range(2):
                    halo_copy(a, c, s, way).wait_recv()
        stage(c, 0)
        stage(c, views + 1)
        compute(c, 0)
        if views > 1:
            compute(c, views - 1)
        for a, (sums, edge) in enumerate(((ak, hk), (av, hv))):
            for way, w in enumerate((0, views + 1)):
                for s in range(parts):
                    edge[c, way, s] = sums[w, s * PAD : s * PAD + toks].astype(BF16)
                part_copy(a, c, way).start()
        for a in range(2):
            for s in range(1, parts):
                out_copy(a, c, s).start()
        finish(c, ak, av)

    @pl.loop(0, chunks)
    def _(c):
        for a in range(4):
            for s in range(1, parts):
                in_copy(a, c, s).wait_send()
                out_copy(a, c, s).wait_send()
                out_arrival(a, c, s).wait_recv()
        for a in range(2):
            for way in range(2):
                part_copy(a, c, way).wait_send()
                for s in range(parts):
                    halo_copy(a, c, s, way).wait_send()


def solution(mesh):
    groups, parts = mesh.shape["view"], mesh.shape["tok"]

    def local(queries, keys, values, grad_out):
        views, toks, width = queries.shape
        lanes = 2 * (width // HEADS)
        chunks = width // parts // lanes
        vmem = pltpu.VMEM
        dma = pltpu.SemaphoreType.DMA
        part = vmem((chunks, parts, views, toks, lanes), BF16)
        wide = vmem((chunks, parts, views + 2, toks, lanes), BF16)
        edge = vmem((chunks, 2, parts, toks, lanes), BF16)
        rows = vmem((views + 2, parts * PAD, lanes), BF16)
        cols = vmem((views + 2, lanes, parts * PAD), BF16)
        sums = vmem((views + 2, parts * PAD, lanes), F32)
        shape = jax.ShapeDtypeStruct(queries.shape, BF16)
        flops = 12 * views * parts * toks * 3 * parts * toks * (width // parts)
        return pl.pallas_call(
            functools.partial(kernel, groups, parts),
            out_shape=(shape,) * 4,
            in_specs=[pl.BlockSpec(memory_space=pltpu.VMEM)] * 4,
            out_specs=[pl.BlockSpec(memory_space=pltpu.VMEM)] * 4,
            scratch_shapes=[
                part, part, wide, wide, part, part, part, part, edge, edge, edge, edge,
                rows, rows, cols, cols, sums, sums,
                dma((chunks, parts, 4)), dma((chunks, parts, 4)), dma((chunks, 4)),
                dma((chunks, parts, 2, 2)), dma((chunks, parts, 2, 2)),
                dma((chunks, 2, 2)), dma((chunks, 2, 2)),
                dma((chunks, parts, 4)), dma((chunks, parts, 4)),
            ],
            cost_estimate=pl.CostEstimate(
                flops=flops, bytes_accessed=16 * views * toks * width, transcendentals=0
            ),
            compiler_params=pltpu.CompilerParams(
                collective_id=0, has_side_effects=True, vmem_limit_bytes=48 * 1024 * 1024
            ),
        )(queries, keys, values, grad_out)

    spec = P("view", "tok", None)
    return jax.shard_map(
        local, mesh=mesh, in_specs=(spec,) * 4, out_specs=(spec,) * 4, check_vma=False
    )
```

```python
import functools
import math

import jax
import jax.numpy as jnp
from jax import lax
from jax.experimental import pallas as pl
from jax.experimental.pallas import tpu as pltpu
from jax.sharding import PartitionSpec as P

HEADS = 16
PAD = 64
NEG = -1e30
MESH = pl.DeviceIdType.MESH
F32 = jnp.float32
BF16 = jnp.bfloat16


def kernel(
    groups, parts, q_ref, k_ref, v_ref, g_ref, o_ref, dq_ref, dk_ref, dv_ref,
    qb, gb, kvb, ob, dqb, dkb, dvb, edge, got,
    kp, vp, kt, vt, ak, av,
    in_send, in_recv, own_sem, halo_send, halo_recv, part_send, part_recv, out_send, out_recv,
):
    views, toks, width = q_ref.shape
    lanes = kp.shape[-1]
    half = lanes // 2
    share = width // parts
    chunks = share // lanes
    scale = 1.0 / math.sqrt(half)
    log2e = math.log2(math.e)
    whole8 = toks // 8 * 8
    up8 = (toks + 7) // 8 * 8
    me_v = lax.axis_index("view")
    me_t = lax.axis_index("tok")
    after = lax.rem(me_v + 1, groups)
    before = lax.rem(me_v + groups - 1, groups)
    peers = [lax.rem(me_t + s, parts) for s in range(parts)]

    barrier = pltpu.get_barrier_semaphore()
    for dev in [(before, me_t), (after, me_t)] + [(me_v, p) for p in peers[1:]]:
        pl.semaphore_signal(barrier, inc=1, device_id=dev, device_id_type=MESH)
    pl.semaphore_wait(barrier, parts + 1)

    def span(owner, c):
        return pl.ds(pl.multiple_of(owner * share + c * lanes, lanes), lanes)

    ins = (q_ref, g_ref, k_ref, v_ref)

    def landing(a, c, s):
        if a < 2:
            return (qb, gb)[a].at[c, s]
        return kvb.at[c, pl.ds(1, views), s, a - 2]

    def in_copy(a, c, s):
        return pltpu.make_async_remote_copy(
            src_ref=ins[a].at[:, :, span(peers[s], c)],
            dst_ref=landing(a, c, parts - s),
            send_sem=in_send.at[c, s, a],
            recv_sem=in_recv.at[c, parts - s, a],
            device_id=(me_v, peers[s]),
            device_id_type=MESH,
        )

    def own_copy(a, c):
        return pltpu.make_async_copy(
            ins[a].at[:, :, span(me_t, c)], landing(a, c, 0), own_sem.at[c, a]
        )

    def halo_copy(c, late, way):
        slots = pl.ds(1, parts - 1) if late else pl.ds(0, 1)
        src, dst, dev = ((1, views + 1, before), (views, 0, after))[way]
        return pltpu.make_async_remote_copy(
            src_ref=kvb.at[c, src, slots],
            dst_ref=kvb.at[c, dst, slots],
            send_sem=halo_send.at[c, late, way],
            recv_sem=halo_recv.at[c, late, way],
            device_id=(dev, me_t),
            device_id_type=MESH,
        )

    def part_copy(c, way):
        return pltpu.make_async_remote_copy(
            src_ref=edge.at[c, way],
            dst_ref=got.at[c, way],
            send_sem=part_send.at[c, way],
            recv_sem=part_recv.at[c, way],
            device_id=((before, after)[way], me_t),
            device_id_type=MESH,
        )

    outs = (o_ref, dq_ref, dk_ref, dv_ref)

    def out_copy(a, c, s):
        return pltpu.make_async_remote_copy(
            src_ref=(ob, dqb, dkb, dvb)[a].at[c, s],
            dst_ref=outs[a].at[:, :, span(me_t, c)],
            send_sem=out_send.at[c, s, a],
            recv_sem=out_recv.at[c, parts - s, a],
            device_id=(me_v, peers[s]),
            device_id_type=MESH,
        )

    def out_arrival(a, c, s):
        return pltpu.make_async_remote_copy(
            src_ref=(ob, dqb, dkb, dvb)[a].at[c, s],
            dst_ref=outs[a].at[:, :, span(peers[s], c)],
            send_sem=out_send.at[c, s, a],
            recv_sem=out_recv.at[c, s, a],
            device_id=(me_v, peers[s]),
            device_id_type=MESH,
        )

    def send_in(pair, c):
        for s in range(1, parts):
            for a in pair:
                in_copy(a, c, s).start()

    for a in (2, 3):
        own_copy(a, 0).start()
    send_in((2, 3), 0)
    for a in (0, 1):
        own_copy(a, 0).start()
    send_in((0, 1), 0)
    if chunks > 1:
        send_in((2, 3), 1)

    @pl.loop(1, chunks)
    def _(c):
        @pl.when(c + 1 < chunks)
        def _():
            send_in((2, 3), c + 1)

        send_in((0, 1), c)
        for a in (2, 3, 0, 1):
            own_copy(a, c).start()

    @pl.loop(0, chunks)
    def _(c):
        for a in (2, 3):
            own_copy(a, c).wait()
        for way in range(2):
            halo_copy(c, 0, way).start()

    def relay(c):
        for s in range(1, parts):
            for a in (2, 3):
                in_copy(a, c, parts - s).wait_recv()
        for way in range(2):
            halo_copy(c, 1, way).start()

    def queries_ready(c):
        for a in (0, 1):
            own_copy(a, c).wait()
            for s in range(1, parts):
                in_copy(a, c, parts - s).wait_recv()

    def pad(x):
        return jnp.concatenate([x, jnp.zeros((PAD - toks, lanes), x.dtype)], axis=0)

    def stage(c, w):
        for a, rows, cols in ((0, kp, kt), (1, vp, vt)):
            block = jnp.concatenate([pad(kvb[c, w, s, a]) for s in range(parts)], axis=0)
            rows[w] = block
            cols[w] = block.T

    def stage_own(c):
        for w in range(1, views + 1):
            stage(c, w)

    def stage_halo(c):
        for late in range(2):
            for way in range(2):
                halo_copy(c, late, way).wait_recv()
        stage(c, 0)
        stage(c, views + 1)

    lane = lax.broadcasted_iota(jnp.int32, (2 * PAD, lanes), 1)
    row_ok = lax.broadcasted_iota(jnp.int32, (up8 - whole8, 2 * lanes), 0) < toks - whole8
    blocks = 3 * parts

    def twin(x):
        zero = jnp.zeros_like(x)
        return jnp.concatenate([jnp.where(lane < half, x, zero), jnp.where(lane < half, zero, x)], 0)

    def full(x):
        filler = jnp.zeros((blocks, PAD - up8, 2 * lanes), F32)
        return jnp.concatenate([x, filler], axis=1).reshape(blocks * PAD, 2 * lanes).astype(BF16)

    def diagonal(x):
        return jnp.concatenate([x[:half, :lanes], x[half:, lanes:]], axis=0).T

    def dot(x, y):
        return jnp.dot(x, y, preferred_element_type=F32)

    def dot_t(x, y):
        return lax.dot_general(x, y, (((1,), (1,)), ((), ())), preferred_element_type=F32)

    def compute(c, v):
        now = lax.rem(c, 2)
        key_rows = kp[v : v + 3].reshape(blocks * PAD, lanes)
        value_rows = vp[v : v + 3].reshape(blocks * PAD, lanes)
        key_cols = jnp.concatenate([kt[v + j] for j in range(3)], axis=1)
        value_cols = jnp.concatenate([vt[v + j] for j in range(3)], axis=1)
        for s in range(0, parts, 2):
            query = jnp.concatenate([pad(qb[c, s + i, v]) for i in range(2)], axis=0)
            grad = jnp.concatenate([pad(gb[c, s + i, v]) for i in range(2)], axis=0)
            query = twin(query * jnp.asarray(scale, BF16))
            grad = twin(grad)
            scores = dot_t(key_rows, query).reshape(blocks, PAD, 2 * lanes)
            tail = jnp.where(row_ok[None], scores[:, whole8:up8], NEG)
            scores = jnp.concatenate([scores[:, :whole8], tail], axis=1)
            top = jnp.max(scores, axis=(0, 1), keepdims=True)
            probs = jnp.exp2((scores - top) * log2e)
            probs = probs * (1.0 / jnp.sum(probs, axis=(0, 1), keepdims=True))
            grad_probs = dot_t(value_rows, grad).reshape(blocks, PAD, 2 * lanes)[:, :up8]
            weighted = probs * grad_probs
            delta = jnp.sum(weighted, axis=(0, 1), keepdims=True)
            probs_bf = full(probs)
            grad_bf = full(weighted - probs * delta)
            key_term = dot(grad_bf, query).reshape(3, parts * PAD, lanes)
            value_term = dot(probs_bf, grad).reshape(3, parts * PAD, lanes)
            ak[now, v : v + 3] += key_term
            av[now, v : v + 3] += value_term
            attended = diagonal(dot(value_cols, probs_bf)).astype(BF16)
            query_grad = (diagonal(dot(key_cols, grad_bf)) * scale).astype(BF16)
            for i in range(2):
                rows = slice(i * PAD, i * PAD + toks)
                if s + i == 0:
                    o_ref[v, :, span(me_t, c)] = attended[rows]
                    dq_ref[v, :, span(me_t, c)] = query_grad[rows]
                else:
                    ob[c, s + i, v] = attended[rows]
                    dqb[c, s + i, v] = query_grad[rows]

    def clear(c):
        now = lax.rem(c, 2)
        ak[now] = jnp.zeros(ak.shape[1:], F32)
        av[now] = jnp.zeros(av.shape[1:], F32)

    def middle(c):
        for v in range(1, views - 1):
            compute(c, v)

    def edges(c):
        compute(c, 0)
        if views > 1:
            compute(c, views - 1)
        now = lax.rem(c, 2)
        for way, w in enumerate((0, views + 1)):
            for a, sums in enumerate((ak, av)):
                for s in range(parts):
                    edge[c, way, a, s] = sums[now, w, s * PAD : s * PAD + toks].astype(BF16)
            part_copy(c, way).start()

    def send_rows(c):
        for s in range(1, parts):
            for a in range(2):
                out_copy(a, c, s).start()

    def finish(c):
        now = lax.rem(c, 2)
        for way in range(2):
            part_copy(c, way).wait_recv()
        for a, (sums, buf, ref) in enumerate(((ak, dkb, dk_ref), (av, dvb, dv_ref))):
            for s in reversed(range(parts)):
                for v in range(views):
                    total = sums[now, v + 1, s * PAD : s * PAD + toks]
                    if v == 0:
                        total = total + got[c, 1, a, s].astype(F32)
                    if v == views - 1:
                        total = total + got[c, 0, a, s].astype(F32)
                    if s == 0:
                        ref[v, :, span(me_t, c)] = total.astype(BF16)
                    else:
                        buf[c, s, v] = total.astype(BF16)
                if s > 0:
                    out_copy(2 + a, c, s).start()

    relay(0)
    stage_own(0)
    clear(0)
    queries_ready(0)
    middle(0)
    if chunks > 1:
        relay(1)
    stage_halo(0)
    edges(0)
    send_rows(0)

    @pl.loop(1, chunks)
    def _(c):
        stage_own(c)
        clear(c)

        @pl.when(c + 1 < chunks)
        def _():
            relay(c + 1)

        queries_ready(c)
        stage_halo(c)
        edges(c)
        finish(c - 1)
        middle(c)
        send_rows(c)

    finish(chunks - 1)

    @pl.loop(0, chunks)
    def _(c):
        for a in range(4):
            for s in range(1, parts):
                in_copy(a, c, s).wait_send()
                out_copy(a, c, s).wait_send()
                out_arrival(a, c, s).wait_recv()
        for way in range(2):
            part_copy(c, way).wait_send()
            for late in range(2):
                halo_copy(c, late, way).wait_send()


def deliver(*refs):
    count = len(refs) // 2
    copies = [
        pltpu.make_async_copy(refs[i], refs[count + i], refs[-1].at[i]) for i in range(count)
    ]
    for copy in copies:
        copy.start()
    for copy in copies:
        copy.wait()


def solution(mesh):
    groups, parts = mesh.shape["view"], mesh.shape["tok"]

    def local(queries, keys, values, grad_out):
        views, toks, width = queries.shape
        lanes = 2 * (width // HEADS)
        chunks = width // parts // lanes
        vmem = pltpu.VMEM
        dma = pltpu.SemaphoreType.DMA
        part = vmem((chunks, parts, views, toks, lanes), BF16)
        pairs = vmem((chunks, views + 2, parts, 2, toks, lanes), BF16)
        edge = vmem((chunks, 2, 2, parts, toks, lanes), BF16)
        rows = vmem((views + 2, parts * PAD, lanes), BF16)
        cols = vmem((views + 2, lanes, parts * PAD), BF16)
        sums = vmem((2, views + 2, parts * PAD, lanes), F32)
        shape = jax.ShapeDtypeStruct(queries.shape, BF16)
        flops = 12 * views * parts * toks * 3 * parts * toks * (width // parts)
        results = pl.pallas_call(
            functools.partial(kernel, groups, parts),
            out_shape=(shape,) * 4,
            in_specs=[pl.BlockSpec(memory_space=pl.ANY)] * 4,
            out_specs=[pl.BlockSpec(memory_space=pltpu.VMEM)] * 4,
            scratch_shapes=[
                part, part, pairs, part, part, part, part, edge, edge,
                rows, rows, cols, cols, sums, sums,
                dma((chunks, parts, 4)), dma((chunks, parts, 4)), dma((chunks, 4)),
                dma((chunks, 2, 2)), dma((chunks, 2, 2)),
                dma((chunks, 2)), dma((chunks, 2)),
                dma((chunks, parts, 4)), dma((chunks, parts, 4)),
            ],
            cost_estimate=pl.CostEstimate(
                flops=flops, bytes_accessed=16 * views * toks * width, transcendentals=0
            ),
            compiler_params=pltpu.CompilerParams(
                collective_id=0, has_side_effects=True, vmem_limit_bytes=58 * 1024 * 1024
            ),
        )(queries, keys, values, grad_out)
        return pl.pallas_call(
            deliver,
            out_shape=(shape,) * 4,
            in_specs=[pl.BlockSpec(memory_space=pl.ANY)] * 4,
            out_specs=[pl.BlockSpec(memory_space=pl.ANY)] * 4,
            scratch_shapes=[dma((4,))],
            compiler_params=pltpu.CompilerParams(vmem_limit_bytes=58 * 1024 * 1024),
        )(*results)

    spec = P("view", "tok", None)
    return jax.shard_map(
        local, mesh=mesh, in_specs=(spec,) * 4, out_specs=(spec,) * 4, check_vma=False
    )
```

```python
import functools
import math

import jax
import jax.numpy as jnp
from jax import lax
from jax.experimental import pallas as pl
from jax.experimental.pallas import tpu as pltpu
from jax.sharding import PartitionSpec as P

HEADS = 16
PAD = 64
NEG = -1e30
MESH = pl.DeviceIdType.MESH
F32 = jnp.float32
BF16 = jnp.bfloat16


def kernel(
    groups, parts, q_ref, k_ref, v_ref, g_ref, o_ref, dq_ref, dk_ref, dv_ref,
    qb, gb, kvb, ob, dqb, dkb, dvb, edge, got,
    kp, vp, kt, vt, ak, av,
    in_send, in_recv, own_sem, halo_send, halo_recv, part_send, part_recv, out_send, out_recv,
):
    views, toks, width = q_ref.shape
    lanes = kp.shape[-1]
    half = lanes // 2
    share = width // parts
    chunks = share // lanes
    scale = 1.0 / math.sqrt(half)
    log2e = math.log2(math.e)
    whole8 = toks // 8 * 8
    up8 = (toks + 7) // 8 * 8
    me_v = lax.axis_index("view")
    me_t = lax.axis_index("tok")
    after = lax.rem(me_v + 1, groups)
    before = lax.rem(me_v + groups - 1, groups)
    peers = [lax.rem(me_t + s, parts) for s in range(parts)]

    barrier = pltpu.get_barrier_semaphore()
    for dev in [(before, me_t), (after, me_t)] + [(me_v, p) for p in peers[1:]]:
        pl.semaphore_signal(barrier, inc=1, device_id=dev, device_id_type=MESH)
    pl.semaphore_wait(barrier, parts + 1)

    def span(owner, c):
        return pl.ds(pl.multiple_of(owner * share + c * lanes, lanes), lanes)

    ins = (q_ref, g_ref, k_ref, v_ref)

    def landing(a, c, s):
        if a < 2:
            return (qb, gb)[a].at[c, s]
        return kvb.at[c, pl.ds(1, views), s, a - 2]

    def in_copy(a, c, s):
        return pltpu.make_async_remote_copy(
            src_ref=ins[a].at[:, :, span(peers[s], c)],
            dst_ref=landing(a, c, parts - s),
            send_sem=in_send.at[c, s, a],
            recv_sem=in_recv.at[c, parts - s, a],
            device_id=(me_v, peers[s]),
            device_id_type=MESH,
        )

    def own_copy(a, c):
        return pltpu.make_async_copy(
            ins[a].at[:, :, span(me_t, c)], landing(a, c, 0), own_sem.at[c, a]
        )

    def halo_copy(c, late, way):
        slots = pl.ds(1, parts - 1) if late else pl.ds(0, 1)
        src, dst, dev = ((1, views + 1, before), (views, 0, after))[way]
        return pltpu.make_async_remote_copy(
            src_ref=kvb.at[c, src, slots],
            dst_ref=kvb.at[c, dst, slots],
            send_sem=halo_send.at[c, late, way],
            recv_sem=halo_recv.at[c, late, way],
            device_id=(dev, me_t),
            device_id_type=MESH,
        )

    def part_copy(c, way):
        return pltpu.make_async_remote_copy(
            src_ref=edge.at[c, way],
            dst_ref=got.at[c, way],
            send_sem=part_send.at[c, way],
            recv_sem=part_recv.at[c, way],
            device_id=((before, after)[way], me_t),
            device_id_type=MESH,
        )

    outs = (o_ref, dq_ref, dk_ref, dv_ref)

    def out_copy(a, c, s):
        return pltpu.make_async_remote_copy(
            src_ref=(ob, dqb, dkb, dvb)[a].at[c, s],
            dst_ref=outs[a].at[:, :, span(me_t, c)],
            send_sem=out_send.at[c, s, a],
            recv_sem=out_recv.at[c, parts - s, a],
            device_id=(me_v, peers[s]),
            device_id_type=MESH,
        )

    def out_arrival(a, c, s):
        return pltpu.make_async_remote_copy(
            src_ref=(ob, dqb, dkb, dvb)[a].at[c, s],
            dst_ref=outs[a].at[:, :, span(peers[s], c)],
            send_sem=out_send.at[c, s, a],
            recv_sem=out_recv.at[c, s, a],
            device_id=(me_v, peers[s]),
            device_id_type=MESH,
        )

    def send_in(pair, c):
        for s in range(1, parts):
            for a in pair:
                in_copy(a, c, s).start()

    for a in (2, 3):
        own_copy(a, 0).start()
    send_in((2, 3), 0)
    for a in (0, 1):
        own_copy(a, 0).start()
    send_in((0, 1), 0)
    if chunks > 1:
        send_in((2, 3), 1)

    @pl.loop(1, chunks)
    def _(c):
        @pl.when(c + 1 < chunks)
        def _():
            send_in((2, 3), c + 1)

        send_in((0, 1), c)
        for a in (2, 3, 0, 1):
            own_copy(a, c).start()

    @pl.loop(0, chunks)
    def _(c):
        for a in (2, 3):
            own_copy(a, c).wait()
        for way in range(2):
            halo_copy(c, 0, way).start()

    def relay(c):
        for s in range(1, parts):
            for a in (2, 3):
                in_copy(a, c, parts - s).wait_recv()
        for way in range(2):
            halo_copy(c, 1, way).start()

    def queries_ready(c):
        for a in (0, 1):
            own_copy(a, c).wait()
            for s in range(1, parts):
                in_copy(a, c, parts - s).wait_recv()

    def pad(x):
        return jnp.concatenate([x, jnp.zeros((PAD - toks, lanes), x.dtype)], axis=0)

    def stage(c, w):
        for a, rows, cols in ((0, kp, kt), (1, vp, vt)):
            block = jnp.concatenate([pad(kvb[c, w, s, a]) for s in range(parts)], axis=0)
            rows[w] = block
            cols[w] = block.T

    def stage_own(c):
        for w in range(1, views + 1):
            stage(c, w)

    def stage_halo(c):
        for late in range(2):
            for way in range(2):
                halo_copy(c, late, way).wait_recv()
        stage(c, 0)
        stage(c, views + 1)

    lane = lax.broadcasted_iota(jnp.int32, (2 * PAD, lanes), 1)
    row_ok = lax.broadcasted_iota(jnp.int32, (up8 - whole8, 2 * lanes), 0) < toks - whole8
    blocks = 3 * parts

    def twin(x):
        zero = jnp.zeros_like(x)
        return jnp.concatenate([jnp.where(lane < half, x, zero), jnp.where(lane < half, zero, x)], 0)

    def full(x):
        filler = jnp.zeros((blocks, PAD - up8, 2 * lanes), F32)
        return jnp.concatenate([x, filler], axis=1).reshape(blocks * PAD, 2 * lanes).astype(BF16)

    def diagonal(x):
        return jnp.concatenate([x[:half, :lanes], x[half:, lanes:]], axis=0).T

    def dot(x, y):
        return jnp.dot(x, y, preferred_element_type=F32)

    def dot_t(x, y):
        return lax.dot_general(x, y, (((1,), (1,)), ((), ())), preferred_element_type=F32)

    def compute(c, v):
        now = lax.rem(c, 2)
        key_rows = kp[v : v + 3].reshape(blocks * PAD, lanes)
        value_rows = vp[v : v + 3].reshape(blocks * PAD, lanes)
        key_cols = jnp.concatenate([kt[v + j] for j in range(3)], axis=1)
        value_cols = jnp.concatenate([vt[v + j] for j in range(3)], axis=1)
        for s in range(0, parts, 2):
            query = jnp.concatenate([pad(qb[c, s + i, v]) for i in range(2)], axis=0)
            grad = jnp.concatenate([pad(gb[c, s + i, v]) for i in range(2)], axis=0)
            query = twin(query * jnp.asarray(scale, BF16))
            grad = twin(grad)
            scores = dot_t(key_rows, query).reshape(blocks, PAD, 2 * lanes)
            tail = jnp.where(row_ok[None], scores[:, whole8:up8], NEG)
            scores = jnp.concatenate([scores[:, :whole8], tail], axis=1)
            top = jnp.max(scores, axis=(0, 1), keepdims=True)
            probs = jnp.exp2((scores - top) * log2e)
            probs = probs * (1.0 / jnp.sum(probs, axis=(0, 1), keepdims=True))
            grad_probs = dot_t(value_rows, grad).reshape(blocks, PAD, 2 * lanes)[:, :up8]
            weighted = probs * grad_probs
            delta = jnp.sum(weighted, axis=(0, 1), keepdims=True)
            probs_bf = full(probs)
            grad_bf = full(weighted - probs * delta)
            key_term = dot(grad_bf, query).reshape(3, parts * PAD, lanes)
            value_term = dot(probs_bf, grad).reshape(3, parts * PAD, lanes)
            ak[now, v : v + 3] += key_term
            av[now, v : v + 3] += value_term
            attended = diagonal(dot(value_cols, probs_bf)).astype(BF16)
            query_grad = (diagonal(dot(key_cols, grad_bf)) * scale).astype(BF16)
            for i in range(2):
                rows = slice(i * PAD, i * PAD + toks)
                if s + i == 0:
                    o_ref[v, :, span(me_t, c)] = attended[rows]
                    dq_ref[v, :, span(me_t, c)] = query_grad[rows]
                else:
                    ob[c, s + i, v] = attended[rows]
                    dqb[c, s + i, v] = query_grad[rows]

    def clear(c):
        now = lax.rem(c, 2)
        ak[now] = jnp.zeros(ak.shape[1:], F32)
        av[now] = jnp.zeros(av.shape[1:], F32)

    def middle(c):
        for v in range(1, views - 1):
            compute(c, v)

    def edges(c):
        compute(c, 0)
        if views > 1:
            compute(c, views - 1)
        now = lax.rem(c, 2)
        for way, w in enumerate((0, views + 1)):
            for a, sums in enumerate((ak, av)):
                for s in range(parts):
                    edge[c, way, a, s] = sums[now, w, s * PAD : s * PAD + toks].astype(BF16)
            part_copy(c, way).start()

    def send_rows(c):
        for s in range(1, parts):
            for a in range(2):
                out_copy(a, c, s).start()

    def finish(c):
        now = lax.rem(c, 2)
        for way in range(2):
            part_copy(c, way).wait_recv()
        for a, (sums, buf, ref) in enumerate(((ak, dkb, dk_ref), (av, dvb, dv_ref))):
            for s in reversed(range(parts)):
                for v in range(views):
                    total = sums[now, v + 1, s * PAD : s * PAD + toks]
                    if v == 0:
                        total = total + got[c, 1, a, s].astype(F32)
                    if v == views - 1:
                        total = total + got[c, 0, a, s].astype(F32)
                    if s == 0:
                        ref[v, :, span(me_t, c)] = total.astype(BF16)
                    else:
                        buf[c, s, v] = total.astype(BF16)
                if s > 0:
                    out_copy(2 + a, c, s).start()

    relay(0)
    stage_own(0)
    clear(0)
    queries_ready(0)
    middle(0)
    if chunks > 1:
        relay(1)
    stage_halo(0)
    edges(0)
    send_rows(0)

    @pl.loop(1, chunks)
    def _(c):
        stage_own(c)
        clear(c)

        @pl.when(c + 1 < chunks)
        def _():
            relay(c + 1)

        queries_ready(c)
        stage_halo(c)
        edges(c)
        finish(c - 1)
        middle(c)
        send_rows(c)

    finish(chunks - 1)

    @pl.loop(0, chunks)
    def _(c):
        for a in range(4):
            for s in range(1, parts):
                in_copy(a, c, s).wait_send()
                out_copy(a, c, s).wait_send()
                out_arrival(a, c, s).wait_recv()
        for way in range(2):
            part_copy(c, way).wait_send()
            for late in range(2):
                halo_copy(c, late, way).wait_send()


def deliver(*refs):
    count = len(refs) // 2
    copies = [
        pltpu.make_async_copy(refs[i], refs[count + i], refs[-1].at[i]) for i in range(count)
    ]
    for copy in copies:
        copy.start()
    for copy in copies:
        copy.wait()


def solution(mesh):
    groups, parts = mesh.shape["view"], mesh.shape["tok"]

    def local(queries, keys, values, grad_out):
        views, toks, width = queries.shape
        lanes = 2 * (width // HEADS)
        chunks = width // parts // lanes
        vmem = pltpu.VMEM
        dma = pltpu.SemaphoreType.DMA
        part = vmem((chunks, parts, views, toks, lanes), BF16)
        pairs = vmem((chunks, views + 2, parts, 2, toks, lanes), BF16)
        edge = vmem((chunks, 2, 2, parts, toks, lanes), BF16)
        rows = vmem((views + 2, parts * PAD, lanes), BF16)
        cols = vmem((views + 2, lanes, parts * PAD), BF16)
        sums = vmem((2, views + 2, parts * PAD, lanes), F32)
        shape = jax.ShapeDtypeStruct(queries.shape, BF16)
        flops = 12 * views * parts * toks * 3 * parts * toks * (width // parts)
        results = pl.pallas_call(
            functools.partial(kernel, groups, parts),
            out_shape=(vmem(queries.shape, BF16),) * 4,
            in_specs=[pl.BlockSpec(memory_space=pl.ANY)] * 4,
            out_specs=[pl.BlockSpec(memory_space=pltpu.VMEM)] * 4,
            scratch_shapes=[
                part, part, pairs, part, part, part, part, edge, edge,
                rows, rows, cols, cols, sums, sums,
                dma((chunks, parts, 4)), dma((chunks, parts, 4)), dma((chunks, 4)),
                dma((chunks, 2, 2)), dma((chunks, 2, 2)),
                dma((chunks, 2)), dma((chunks, 2)),
                dma((chunks, parts, 4)), dma((chunks, parts, 4)),
            ],
            cost_estimate=pl.CostEstimate(
                flops=flops, bytes_accessed=16 * views * toks * width, transcendentals=0
            ),
            compiler_params=pltpu.CompilerParams(
                collective_id=0, has_side_effects=True, vmem_limit_bytes=58 * 1024 * 1024
            ),
        )(queries, keys, values, grad_out)
        return pl.pallas_call(
            deliver,
            out_shape=(shape,) * 4,
            in_specs=[pl.BlockSpec(memory_space=pltpu.VMEM)] * 4,
            out_specs=[pl.BlockSpec(memory_space=pl.ANY)] * 4,
            scratch_shapes=[dma((4,))],
            compiler_params=pltpu.CompilerParams(vmem_limit_bytes=48 * 1024 * 1024),
        )(*results)

    spec = P("view", "tok", None)
    return jax.shard_map(
        local, mesh=mesh, in_specs=(spec,) * 4, out_specs=(spec,) * 4, check_vma=False
    )
```

```python
import functools
import math

import jax
import jax.numpy as jnp
from jax import lax
from jax.experimental import pallas as pl
from jax.experimental.pallas import tpu as pltpu
from jax.sharding import PartitionSpec as P

HEADS = 16
PAD = 64
TILE = 16
NEG = -1e30
MESH = pl.DeviceIdType.MESH
F32 = jnp.float32
BF16 = jnp.bfloat16


def kernel(
    groups, parts, q_ref, k_ref, v_ref, g_ref, o_ref, dq_ref, dk_ref, dv_ref,
    qx, gx, kx, vx, in_from, in_to, out_from, out_to, tails, edge, got,
    kvp, kvt, ak, av,
    load_sem, in_send, in_recv, halo_send, halo_recv, part_send, part_recv, out_send, out_recv,
):
    views, toks, width = q_ref.shape
    lanes = kvp.shape[-1]
    half = lanes // 2
    share = width // parts
    chunks = share // lanes
    scale = 1.0 / math.sqrt(half)
    log2e = math.log2(math.e)
    whole8 = toks // 8 * 8
    up8 = (toks + 7) // 8 * 8
    bulk = toks // TILE * TILE
    rest = toks - bulk
    base = 2 * views * bulk
    tail_rows = in_from.shape[-2] - base
    me_v = lax.axis_index("view")
    me_t = lax.axis_index("tok")
    after = lax.rem(me_v + 1, groups)
    before = lax.rem(me_v + groups - 1, groups)
    peers = [lax.rem(me_t + s, parts) for s in range(parts)]

    ins = (q_ref, g_ref, k_ref, v_ref)
    loaded = (qx, gx, kx, vx)
    ROWS, PAIRS = 0, 1
    members = ((0, 1), (2, 3))

    def load(a, s):
        lanes_of = pl.ds(pl.multiple_of(peers[s] * share, lanes), share)
        return pltpu.make_async_copy(
            ins[a].at[:, :, lanes_of], loaded[a].at[s], load_sem.at[s, a]
        )

    for kind in (PAIRS, ROWS):
        for s in reversed(range(parts)):
            for a in members[kind]:
                load(a, s).start()

    barrier = pltpu.get_barrier_semaphore()
    for dev in [(before, me_t), (after, me_t)] + [(me_v, p) for p in peers[1:]]:
        pl.semaphore_signal(barrier, inc=1, device_id=dev, device_id_type=MESH)

    def span(owner, c):
        return pl.ds(pl.multiple_of(owner * share + c * lanes, lanes), lanes)

    def column(c):
        return pl.ds(pl.multiple_of(c * lanes, lanes), lanes)

    def in_copy(kind, c, s):
        return pltpu.make_async_remote_copy(
            src_ref=in_from.at[kind, c, s],
            dst_ref=in_to.at[kind, c, parts - s],
            send_sem=in_send.at[c, s, kind],
            recv_sem=in_recv.at[c, parts - s, kind],
            device_id=(me_v, peers[s]),
            device_id_type=MESH,
        )

    def halo_copy(c, way):
        src, dst, dev = ((1, views + 1, before), (views, 0, after))[way]
        return pltpu.make_async_remote_copy(
            src_ref=kvp.at[c, src],
            dst_ref=kvp.at[c, dst],
            send_sem=halo_send.at[c, way],
            recv_sem=halo_recv.at[c, way],
            device_id=(dev, me_t),
            device_id_type=MESH,
        )

    def part_copy(c, way):
        return pltpu.make_async_remote_copy(
            src_ref=edge.at[c, way],
            dst_ref=got.at[c, way],
            send_sem=part_send.at[c, way],
            recv_sem=part_recv.at[c, way],
            device_id=((before, after)[way], me_t),
            device_id_type=MESH,
        )

    outs = (o_ref, dq_ref, dk_ref, dv_ref)

    def out_copy(kind, c, s):
        return pltpu.make_async_remote_copy(
            src_ref=out_from.at[kind, c, s],
            dst_ref=out_to.at[kind, c, parts - s],
            send_sem=out_send.at[c, s, kind],
            recv_sem=out_recv.at[c, parts - s, kind],
            device_id=(me_v, peers[s]),
            device_id_type=MESH,
        )

    tail_row = lax.broadcasted_iota(jnp.int32, (tail_rows, lanes), 0)

    def send_in(kind, c):
        for s in range(1, parts):
            tail = jnp.zeros((tail_rows, lanes), F32)
            for i, a in enumerate(members[kind]):
                for v in range(views):
                    at = i * views + v
                    block = loaded[a][s, v, :, column(c)]
                    in_from[kind, c, s, at * bulk : (at + 1) * bulk] = block[:bulk]
                    for r in range(rest):
                        row = block[bulk + r : bulk + r + 1].astype(F32)
                        tail = jnp.where(tail_row == at * rest + r, row, tail)
            in_from[kind, c, s, base:] = tail.astype(BF16)
            in_copy(kind, c, s).start()

    for kind in (PAIRS, ROWS):
        for s in reversed(range(1, parts)):
            for a in members[kind]:
                load(a, s).wait()
        if kind == PAIRS:
            pl.semaphore_wait(barrier, parts + 1)
        send_in(kind, 0)
    if chunks > 1:
        send_in(PAIRS, 1)

    @pl.loop(1, chunks)
    def _(c):
        @pl.when(c + 1 < chunks)
        def _():
            send_in(PAIRS, c + 1)

        send_in(ROWS, c)

    for a in range(4):
        load(a, 0).wait()

    pad_row = lax.broadcasted_iota(jnp.int32, (PAD - bulk, lanes), 0)

    def blocks_of(kind, i, c, s, v):
        if s == 0:
            block = loaded[members[kind][i]][0, v, :, column(c)]
            return jnp.concatenate([block, jnp.zeros((PAD - toks, lanes), BF16)], axis=0)
        at = i * views + v
        tail = in_to[kind, c, s, base:].astype(F32)
        end = jnp.zeros((PAD - bulk, lanes), F32)
        for r in range(rest):
            end = jnp.where(pad_row == r, tail[at * rest + r : at * rest + r + 1], end)
        main = in_to[kind, c, s, at * bulk : (at + 1) * bulk]
        return jnp.concatenate([main, end.astype(BF16)], axis=0)

    def relay(c):
        for s in range(1, parts):
            in_copy(PAIRS, c, parts - s).wait_recv()
        for v in range(views):
            for a in range(2):
                rows = [blocks_of(PAIRS, a, c, s, v) for s in range(parts)]
                kvp[c, v + 1, a] = jnp.concatenate(rows, axis=0)
        for way in range(2):
            halo_copy(c, way).start()
        for w in range(1, views + 1):
            turn(c, w)

    def turn(c, w):
        for a in range(2):
            kvt[c, w, a] = kvp[c, w, a].T

    def queries_ready(c):
        for s in range(1, parts):
            in_copy(ROWS, c, parts - s).wait_recv()

    def stage_halo(c):
        for way in range(2):
            halo_copy(c, way).wait_recv()
        turn(c, 0)
        turn(c, views + 1)

    def put(kind, i, c, s, v, block):
        at = i * views + v
        out_from[kind, c, s, at * bulk : (at + 1) * bulk] = block[:bulk].astype(BF16)
        for r in range(rest):
            row = at * rest + r
            tails[kind, s, row : row + 1] = block[bulk + r : bulk + r + 1]

    def send_out(kind, c):
        for s in range(1, parts):
            out_from[kind, c, s, base:] = tails[kind, s].astype(BF16)
            out_copy(kind, c, s).start()

    def take(kind, c, s):
        tail = out_to[kind, c, s, base:].astype(F32)
        for i, ref in enumerate(((o_ref, dq_ref), (dk_ref, dv_ref))[kind]):
            for v in range(views):
                at = i * views + v
                ref[v, :bulk, span(peers[s], c)] = out_to[kind, c, s, at * bulk : (at + 1) * bulk]
                if rest:
                    rows = tail[at * rest : (at + 1) * rest]
                    ref[v, bulk:toks, span(peers[s], c)] = rows.astype(BF16)

    lane = lax.broadcasted_iota(jnp.int32, (2 * PAD, lanes), 1)
    row_ok = lax.broadcasted_iota(jnp.int32, (up8 - whole8, 2 * lanes), 0) < toks - whole8
    blocks = 3 * parts

    def twin(x):
        zero = jnp.zeros_like(x)
        return jnp.concatenate([jnp.where(lane < half, x, zero), jnp.where(lane < half, zero, x)], 0)

    def full(x):
        filler = jnp.zeros((blocks, PAD - up8, 2 * lanes), F32)
        return jnp.concatenate([x, filler], axis=1).reshape(blocks * PAD, 2 * lanes).astype(BF16)

    def diagonal(x):
        return jnp.concatenate([x[:half, :lanes], x[half:, lanes:]], axis=0).T

    def dot(x, y):
        return jnp.dot(x, y, preferred_element_type=F32)

    def dot_t(x, y):
        return lax.dot_general(x, y, (((1,), (1,)), ((), ())), preferred_element_type=F32)

    def compute(c, v):
        now = lax.rem(c, 2)
        key_rows, value_rows = (
            jnp.concatenate([kvp[c, v + j, a] for j in range(3)], axis=0) for a in range(2)
        )
        key_cols, value_cols = (
            jnp.concatenate([kvt[c, v + j, a] for j in range(3)], axis=1) for a in range(2)
        )
        for s in range(0, parts, 2):
            query = jnp.concatenate([blocks_of(ROWS, 0, c, s + i, v) for i in range(2)], axis=0)
            grad = jnp.concatenate([blocks_of(ROWS, 1, c, s + i, v) for i in range(2)], axis=0)
            query = twin(query * jnp.asarray(scale, BF16))
            grad = twin(grad)
            scores = dot_t(key_rows, query).reshape(blocks, PAD, 2 * lanes)
            tail = jnp.where(row_ok[None], scores[:, whole8:up8], NEG)
            scores = jnp.concatenate([scores[:, :whole8], tail], axis=1)
            top = jnp.max(scores, axis=(0, 1), keepdims=True)
            probs = jnp.exp2((scores - top) * log2e)
            probs = probs * (1.0 / jnp.sum(probs, axis=(0, 1), keepdims=True))
            grad_probs = dot_t(value_rows, grad).reshape(blocks, PAD, 2 * lanes)[:, :up8]
            weighted = probs * grad_probs
            delta = jnp.sum(weighted, axis=(0, 1), keepdims=True)
            probs_bf = full(probs)
            grad_bf = full(weighted - probs * delta)
            key_term = dot(grad_bf, query).reshape(3, parts * PAD, lanes)
            value_term = dot(probs_bf, grad).reshape(3, parts * PAD, lanes)
            ak[now, v : v + 3] += key_term
            av[now, v : v + 3] += value_term
            attended = diagonal(dot(value_cols, probs_bf))
            query_grad = diagonal(dot(key_cols, grad_bf)) * scale
            for i in range(2):
                rows = slice(i * PAD, i * PAD + toks)
                if s + i == 0:
                    o_ref[v, :, span(me_t, c)] = attended[rows].astype(BF16)
                    dq_ref[v, :, span(me_t, c)] = query_grad[rows].astype(BF16)
                else:
                    put(ROWS, 0, c, s + i, v, attended[rows])
                    put(ROWS, 1, c, s + i, v, query_grad[rows])

    def clear(c):
        now = lax.rem(c, 2)
        ak[now] = jnp.zeros(ak.shape[1:], F32)
        av[now] = jnp.zeros(av.shape[1:], F32)

    def middle(c):
        for v in range(1, views - 1):
            compute(c, v)

    def edges(c):
        compute(c, 0)
        if views > 1:
            compute(c, views - 1)
        now = lax.rem(c, 2)
        for way, w in enumerate((0, views + 1)):
            for a, sums in enumerate((ak, av)):
                for s in range(parts):
                    edge[c, way, a, s] = sums[now, w, s * PAD : s * PAD + toks].astype(BF16)
            part_copy(c, way).start()

    def finish(c):
        now = lax.rem(c, 2)
        for way in range(2):
            part_copy(c, way).wait_recv()
        for s in reversed(range(parts)):
            for a, (sums, ref) in enumerate(((ak, dk_ref), (av, dv_ref))):
                for v in range(views):
                    total = sums[now, v + 1, s * PAD : s * PAD + toks]
                    if v == 0:
                        total = total + got[c, 1, a, s].astype(F32)
                    if v == views - 1:
                        total = total + got[c, 0, a, s].astype(F32)
                    if s == 0:
                        ref[v, :, span(me_t, c)] = total.astype(BF16)
                    else:
                        put(PAIRS, a, c, s, v, total)
            if s == 1:
                send_out(PAIRS, c)

    tails[...] = jnp.zeros_like(tails)
    relay(0)
    clear(0)
    queries_ready(0)
    middle(0)
    if chunks > 1:
        relay(1)
    stage_halo(0)
    edges(0)
    send_out(ROWS, 0)

    @pl.loop(1, chunks)
    def _(c):
        clear(c)

        @pl.when(c + 1 < chunks)
        def _():
            relay(c + 1)

        queries_ready(c)
        stage_halo(c)
        edges(c)
        finish(c - 1)
        middle(c)
        send_out(ROWS, c)

    finish(chunks - 1)

    @pl.loop(0, chunks)
    def _(c):
        for kind in range(2):
            for s in range(1, parts):
                in_copy(kind, c, s).wait_send()
                out_copy(kind, c, s).wait_send()
                out_copy(kind, c, parts - s).wait_recv()
                take(kind, c, s)
        for way in range(2):
            part_copy(c, way).wait_send()
            halo_copy(c, way).wait_send()


def deliver(*refs):
    count = len(refs) // 2
    copies = [
        pltpu.make_async_copy(refs[i], refs[count + i], refs[-1].at[i]) for i in range(count)
    ]
    for copy in copies:
        copy.start()
    for copy in copies:
        copy.wait()


def solution(mesh):
    groups, parts = mesh.shape["view"], mesh.shape["tok"]

    def local(queries, keys, values, grad_out):
        views, toks, width = queries.shape
        lanes = 2 * (width // HEADS)
        chunks = width // parts // lanes
        vmem = pltpu.VMEM
        dma = pltpu.SemaphoreType.DMA
        bulk = toks // TILE * TILE
        tail = (2 * views * (toks - bulk) + TILE - 1) // TILE * TILE
        source = vmem((parts, views, toks, width // parts), BF16)
        packed = vmem((2, chunks, parts, 2 * views * bulk + tail, lanes), BF16)
        edge = vmem((chunks, 2, 2, parts, toks, lanes), BF16)
        rows = vmem((chunks, views + 2, 2, parts * PAD, lanes), BF16)
        cols = vmem((chunks, views + 2, 2, lanes, parts * PAD), BF16)
        sums = vmem((2, views + 2, parts * PAD, lanes), F32)
        shape = jax.ShapeDtypeStruct(queries.shape, BF16)
        flops = 12 * views * parts * toks * 3 * parts * toks * (width // parts)
        results = pl.pallas_call(
            functools.partial(kernel, groups, parts),
            out_shape=(vmem(queries.shape, BF16),) * 4,
            in_specs=[pl.BlockSpec(memory_space=pl.ANY)] * 4,
            out_specs=[pl.BlockSpec(memory_space=pltpu.VMEM)] * 4,
            scratch_shapes=[
                source, source, source, source, packed, packed, packed, packed,
                vmem((2, parts, tail, lanes), F32), edge, edge, rows, cols, sums, sums,
                dma((parts, 4)), dma((chunks, parts, 2)), dma((chunks, parts, 2)),
                dma((chunks, 2)), dma((chunks, 2)), dma((chunks, 2)), dma((chunks, 2)),
                dma((chunks, parts, 2)), dma((chunks, parts, 2)),
            ],
            cost_estimate=pl.CostEstimate(
                flops=flops, bytes_accessed=16 * views * toks * width, transcendentals=0
            ),
            compiler_params=pltpu.CompilerParams(
                collective_id=0, has_side_effects=True, vmem_limit_bytes=58 * 1024 * 1024
            ),
        )(queries, keys, values, grad_out)
        return pl.pallas_call(
            deliver,
            out_shape=(shape,) * 4,
            in_specs=[pl.BlockSpec(memory_space=pltpu.VMEM)] * 4,
            out_specs=[pl.BlockSpec(memory_space=pl.ANY)] * 4,
            scratch_shapes=[dma((4,))],
            compiler_params=pltpu.CompilerParams(vmem_limit_bytes=48 * 1024 * 1024),
        )(*results)

    spec = P("view", "tok", None)
    return jax.shard_map(
        local, mesh=mesh, in_specs=(spec,) * 4, out_specs=(spec,) * 4, check_vma=False
    )
```

```python
import functools
import math

import jax
import jax.numpy as jnp
from jax import lax
from jax.experimental import pallas as pl
from jax.experimental.pallas import tpu as pltpu
from jax.sharding import PartitionSpec as P

HEADS = 16
PAD = 64
TILE = 16
NEG = -1e30
MESH = pl.DeviceIdType.MESH
F32 = jnp.float32
BF16 = jnp.bfloat16


def kernel(
    groups, parts, q_ref, k_ref, v_ref, g_ref, o_ref, dq_ref, dk_ref, dv_ref,
    qx, gx, kx, vx, in_from, in_to, out_from, out_to, tails, edge, got,
    kvp, kvt, ak, av,
    load_sem, in_send, in_recv, halo_send, halo_recv, part_send, part_recv, out_send, out_recv,
):
    views, toks, width = q_ref.shape
    lanes = kvp.shape[-1]
    half = lanes // 2
    share = width // parts
    chunks = share // lanes
    scale = 1.0 / math.sqrt(half)
    log2e = math.log2(math.e)
    whole8 = toks // 8 * 8
    up8 = (toks + 7) // 8 * 8
    bulk = toks // TILE * TILE
    rest = toks - bulk
    base = 2 * views * bulk
    tail_rows = in_from.shape[-2] - base
    me_v = lax.axis_index("view")
    me_t = lax.axis_index("tok")
    after = lax.rem(me_v + 1, groups)
    before = lax.rem(me_v + groups - 1, groups)
    peers = [lax.rem(me_t + s, parts) for s in range(parts)]

    ins = (q_ref, g_ref, k_ref, v_ref)
    loaded = (qx, gx, kx, vx)
    ROWS, PAIRS = 0, 1
    members = ((0, 1), (2, 3))

    def load(a, s):
        lanes_of = pl.ds(pl.multiple_of(peers[s] * share, lanes), share)
        return pltpu.make_async_copy(
            ins[a].at[:, :, lanes_of], loaded[a].at[s], load_sem.at[s, a]
        )

    for kind in (PAIRS, ROWS):
        for s in reversed(range(parts)):
            for a in members[kind]:
                load(a, s).start()

    barrier = pltpu.get_barrier_semaphore()
    for dev in [(before, me_t), (after, me_t)] + [(me_v, p) for p in peers[1:]]:
        pl.semaphore_signal(barrier, inc=1, device_id=dev, device_id_type=MESH)

    def span(owner, c):
        return pl.ds(pl.multiple_of(owner * share + c * lanes, lanes), lanes)

    def column(c):
        return pl.ds(pl.multiple_of(c * lanes, lanes), lanes)

    def in_copy(kind, c, s):
        return pltpu.make_async_remote_copy(
            src_ref=in_from.at[kind, c, s],
            dst_ref=in_to.at[kind, c, parts - s],
            send_sem=in_send.at[c, s, kind],
            recv_sem=in_recv.at[c, parts - s, kind],
            device_id=(me_v, peers[s]),
            device_id_type=MESH,
        )

    def halo_copy(c, way):
        src, dst, dev = ((1, views + 1, before), (views, 0, after))[way]
        return pltpu.make_async_remote_copy(
            src_ref=kvp.at[c, src],
            dst_ref=kvp.at[c, dst],
            send_sem=halo_send.at[c, way],
            recv_sem=halo_recv.at[c, way],
            device_id=(dev, me_t),
            device_id_type=MESH,
        )

    def part_copy(c, way):
        return pltpu.make_async_remote_copy(
            src_ref=edge.at[c, way],
            dst_ref=got.at[c, way],
            send_sem=part_send.at[c, way],
            recv_sem=part_recv.at[c, way],
            device_id=((before, after)[way], me_t),
            device_id_type=MESH,
        )

    outs = (o_ref, dq_ref, dk_ref, dv_ref)

    def out_copy(kind, c, s):
        return pltpu.make_async_remote_copy(
            src_ref=out_from.at[kind, c, s],
            dst_ref=out_to.at[kind, c, parts - s],
            send_sem=out_send.at[c, s, kind],
            recv_sem=out_recv.at[c, parts - s, kind],
            device_id=(me_v, peers[s]),
            device_id_type=MESH,
        )

    tail_row = lax.broadcasted_iota(jnp.int32, (tail_rows, lanes), 0)

    def send_in(kind, c):
        for s in range(1, parts):
            tail = jnp.zeros((tail_rows, lanes), F32)
            for i, a in enumerate(members[kind]):
                for v in range(views):
                    at = i * views + v
                    block = loaded[a][s, v, :, column(c)]
                    in_from[kind, c, s, at * bulk : (at + 1) * bulk] = block[:bulk]
                    for r in range(rest):
                        row = block[bulk + r : bulk + r + 1].astype(F32)
                        tail = jnp.where(tail_row == at * rest + r, row, tail)
            in_from[kind, c, s, base:] = tail.astype(BF16)
            in_copy(kind, c, s).start()

    for kind in (PAIRS, ROWS):
        for s in reversed(range(1, parts)):
            for a in members[kind]:
                load(a, s).wait()
        if kind == PAIRS:
            pl.semaphore_wait(barrier, parts + 1)
        send_in(kind, 0)
    if chunks > 1:
        send_in(PAIRS, 1)

    @pl.loop(1, chunks)
    def _(c):
        @pl.when(c + 1 < chunks)
        def _():
            send_in(PAIRS, c + 1)

        send_in(ROWS, c)

    for a in range(4):
        load(a, 0).wait()

    pad_row = lax.broadcasted_iota(jnp.int32, (PAD - bulk, lanes), 0)

    def blocks_of(kind, i, c, s, v):
        if s == 0:
            block = loaded[members[kind][i]][0, v, :, column(c)]
            return jnp.concatenate([block, jnp.zeros((PAD - toks, lanes), BF16)], axis=0)
        at = i * views + v
        tail = in_to[kind, c, s, base:].astype(F32)
        end = jnp.zeros((PAD - bulk, lanes), F32)
        for r in range(rest):
            end = jnp.where(pad_row == r, tail[at * rest + r : at * rest + r + 1], end)
        main = in_to[kind, c, s, at * bulk : (at + 1) * bulk]
        return jnp.concatenate([main, end.astype(BF16)], axis=0)

    def relay(c):
        for s in range(1, parts):
            in_copy(PAIRS, c, parts - s).wait_recv()
        for v in range(views):
            for a in range(2):
                rows = [blocks_of(PAIRS, a, c, s, v) for s in range(parts)]
                kvp[c, v + 1, a] = jnp.concatenate(rows, axis=0)
        for way in range(2):
            halo_copy(c, way).start()
        for w in range(1, views + 1):
            turn(c, w)

    def turn(c, w):
        for a in range(2):
            kvt[c, w, a] = kvp[c, w, a].T

    def queries_ready(c):
        for s in range(1, parts):
            in_copy(ROWS, c, parts - s).wait_recv()

    def stage_halo(c):
        for way in range(2):
            halo_copy(c, way).wait_recv()
        turn(c, 0)
        turn(c, views + 1)

    def put(kind, i, c, s, v, block):
        at = i * views + v
        out_from[kind, c, s, at * bulk : (at + 1) * bulk] = block[:bulk].astype(BF16)
        for r in range(rest):
            row = at * rest + r
            tails[kind, s, row : row + 1] = block[bulk + r : bulk + r + 1]

    def send_out(kind, c):
        for s in range(1, parts):
            out_from[kind, c, s, base:] = tails[kind, s].astype(BF16)
            out_copy(kind, c, s).start()

    def take(kind, c, s):
        tail = out_to[kind, c, s, base:].astype(F32)
        for i, ref in enumerate(((o_ref, dq_ref), (dk_ref, dv_ref))[kind]):
            for v in range(views):
                at = i * views + v
                ref[v, :bulk, span(peers[s], c)] = out_to[kind, c, s, at * bulk : (at + 1) * bulk]
                if rest:
                    rows = tail[at * rest : (at + 1) * rest]
                    ref[v, bulk:toks, span(peers[s], c)] = rows.astype(BF16)

    lane = lax.broadcasted_iota(jnp.int32, (2 * PAD, lanes), 1)
    row_ok = lax.broadcasted_iota(jnp.int32, (up8 - whole8, 2 * lanes), 0) < toks - whole8
    blocks = 3 * parts

    def twin(x):
        zero = jnp.zeros_like(x)
        return jnp.concatenate([jnp.where(lane < half, x, zero), jnp.where(lane < half, zero, x)], 0)

    def full(x):
        filler = jnp.zeros((blocks, PAD - up8, 2 * lanes), F32)
        return jnp.concatenate([x, filler], axis=1).reshape(blocks * PAD, 2 * lanes).astype(BF16)

    def diagonal(x):
        return jnp.concatenate([x[:half, :lanes], x[half:, lanes:]], axis=0).T

    def dot(x, y):
        return jnp.dot(x, y, preferred_element_type=F32)

    def dot_t(x, y):
        return lax.dot_general(x, y, (((1,), (1,)), ((), ())), preferred_element_type=F32)

    def front(c, v, s):
        key_rows, value_rows = (
            jnp.concatenate([kvp[c, v + j, a] for j in range(3)], axis=0) for a in range(2)
        )
        query = jnp.concatenate([blocks_of(ROWS, 0, c, s + i, v) for i in range(2)], axis=0)
        grad = jnp.concatenate([blocks_of(ROWS, 1, c, s + i, v) for i in range(2)], axis=0)
        query = twin(query * jnp.asarray(scale, BF16))
        grad = twin(grad)
        scores = dot_t(key_rows, query).reshape(blocks, PAD, 2 * lanes)
        tail = jnp.where(row_ok[None], scores[:, whole8:up8], NEG)
        scores = jnp.concatenate([scores[:, :whole8], tail], axis=1)
        top = jnp.max(scores, axis=(0, 1), keepdims=True)
        probs = jnp.exp2((scores - top) * log2e)
        probs = probs * (1.0 / jnp.sum(probs, axis=(0, 1), keepdims=True))
        grad_probs = dot_t(value_rows, grad).reshape(blocks, PAD, 2 * lanes)[:, :up8]
        weighted = probs * grad_probs
        delta = jnp.sum(weighted, axis=(0, 1), keepdims=True)
        return query, grad, full(probs), full(weighted - probs * delta)

    def back(c, v, s, query, grad, probs_bf, grad_bf):
        now = lax.rem(c, 2)
        key_cols, value_cols = (
            jnp.concatenate([kvt[c, v + j, a] for j in range(3)], axis=1) for a in range(2)
        )
        ak[now, v : v + 3] += dot(grad_bf, query).reshape(3, parts * PAD, lanes)
        av[now, v : v + 3] += dot(probs_bf, grad).reshape(3, parts * PAD, lanes)
        attended = diagonal(dot(value_cols, probs_bf))
        query_grad = diagonal(dot(key_cols, grad_bf)) * scale
        for i in range(2):
            rows = slice(i * PAD, i * PAD + toks)
            if s + i == 0:
                o_ref[v, :, span(me_t, c)] = attended[rows].astype(BF16)
                dq_ref[v, :, span(me_t, c)] = query_grad[rows].astype(BF16)
            else:
                put(ROWS, 0, c, s + i, v, attended[rows])
                put(ROWS, 1, c, s + i, v, query_grad[rows])

    def compute(c, edge_views, inner_views):
        tasks = [(v, s) for v in edge_views + inner_views for s in range(0, parts, 2)]
        last_edge = len(edge_views) * (parts // 2)
        held = None
        for at, (v, s) in enumerate(tasks):
            made = front(c, v, s)
            if held is not None:
                back(c, *tasks[at - 1], *held)
                if at == last_edge:
                    send_parts(c)
            held = made
        if held is not None:
            back(c, *tasks[-1], *held)
        if len(tasks) == last_edge and last_edge:
            send_parts(c)

    def clear(c):
        now = lax.rem(c, 2)
        ak[now] = jnp.zeros(ak.shape[1:], F32)
        av[now] = jnp.zeros(av.shape[1:], F32)

    edge_views = [0, views - 1][: min(views, 2)]
    inner_views = list(range(1, views - 1))

    def send_parts(c):
        now = lax.rem(c, 2)
        for way, w in enumerate((0, views + 1)):
            for a, sums in enumerate((ak, av)):
                for s in range(parts):
                    edge[c, way, a, s] = sums[now, w, s * PAD : s * PAD + toks].astype(BF16)
            part_copy(c, way).start()

    def finish(c):
        now = lax.rem(c, 2)
        for way in range(2):
            part_copy(c, way).wait_recv()
        for s in reversed(range(parts)):
            for a, (sums, ref) in enumerate(((ak, dk_ref), (av, dv_ref))):
                for v in range(views):
                    total = sums[now, v + 1, s * PAD : s * PAD + toks]
                    if v == 0:
                        total = total + got[c, 1, a, s].astype(F32)
                    if v == views - 1:
                        total = total + got[c, 0, a, s].astype(F32)
                    if s == 0:
                        ref[v, :, span(me_t, c)] = total.astype(BF16)
                    else:
                        put(PAIRS, a, c, s, v, total)
            if s == 1:
                send_out(PAIRS, c)

    tails[...] = jnp.zeros_like(tails)
    relay(0)
    clear(0)
    queries_ready(0)
    compute(0, [], inner_views)
    if chunks > 1:
        relay(1)
    stage_halo(0)
    compute(0, edge_views, [])
    send_out(ROWS, 0)

    @pl.loop(1, chunks)
    def _(c):
        clear(c)

        @pl.when(c + 1 < chunks)
        def _():
            relay(c + 1)

        queries_ready(c)
        stage_halo(c)
        compute(c, edge_views, inner_views)
        send_out(ROWS, c)
        finish(c - 1)

    finish(chunks - 1)

    @pl.loop(0, chunks)
    def _(c):
        for kind in range(2):
            for s in range(1, parts):
                in_copy(kind, c, s).wait_send()
                out_copy(kind, c, s).wait_send()
                out_copy(kind, c, parts - s).wait_recv()
                take(kind, c, s)
        for way in range(2):
            part_copy(c, way).wait_send()
            halo_copy(c, way).wait_send()


def deliver(*refs):
    count = len(refs) // 2
    copies = [
        pltpu.make_async_copy(refs[i].at[v], refs[count + i].at[v], refs[-1].at[i, v])
        for i in range(count)
        for v in range(refs[0].shape[0])
    ]
    for copy in copies:
        copy.start()
    for copy in copies:
        copy.wait()


def solution(mesh):
    groups, parts = mesh.shape["view"], mesh.shape["tok"]

    def local(queries, keys, values, grad_out):
        views, toks, width = queries.shape
        lanes = 2 * (width // HEADS)
        chunks = width // parts // lanes
        vmem = pltpu.VMEM
        dma = pltpu.SemaphoreType.DMA
        bulk = toks // TILE * TILE
        tail = (2 * views * (toks - bulk) + 7) // 8 * 8
        source = vmem((parts, views, toks, width // parts), BF16)
        packed = vmem((2, chunks, parts, 2 * views * bulk + tail, lanes), BF16)
        edge = vmem((chunks, 2, 2, parts, toks, lanes), BF16)
        rows = vmem((chunks, views + 2, 2, parts * PAD, lanes), BF16)
        cols = vmem((chunks, views + 2, 2, lanes, parts * PAD), BF16)
        sums = vmem((2, views + 2, parts * PAD, lanes), F32)
        shape = jax.ShapeDtypeStruct(queries.shape, BF16)
        flops = 12 * views * parts * toks * 3 * parts * toks * (width // parts)
        results = pl.pallas_call(
            functools.partial(kernel, groups, parts),
            out_shape=(vmem(queries.shape, BF16),) * 4,
            in_specs=[pl.BlockSpec(memory_space=pl.ANY)] * 4,
            out_specs=[pl.BlockSpec(memory_space=pltpu.VMEM)] * 4,
            scratch_shapes=[
                source, source, source, source, packed, packed, packed, packed,
                vmem((2, parts, tail, lanes), F32), edge, edge, rows, cols, sums, sums,
                dma((parts, 4)), dma((chunks, parts, 2)), dma((chunks, parts, 2)),
                dma((chunks, 2)), dma((chunks, 2)), dma((chunks, 2)), dma((chunks, 2)),
                dma((chunks, parts, 2)), dma((chunks, parts, 2)),
            ],
            cost_estimate=pl.CostEstimate(
                flops=flops, bytes_accessed=16 * views * toks * width, transcendentals=0
            ),
            compiler_params=pltpu.CompilerParams(
                collective_id=0, has_side_effects=True, vmem_limit_bytes=58 * 1024 * 1024
            ),
        )(queries, keys, values, grad_out)
        return pl.pallas_call(
            deliver,
            out_shape=(shape,) * 4,
            in_specs=[pl.BlockSpec(memory_space=pltpu.VMEM)] * 4,
            out_specs=[pl.BlockSpec(memory_space=pl.ANY)] * 4,
            scratch_shapes=[dma((4, views))],
            compiler_params=pltpu.CompilerParams(vmem_limit_bytes=48 * 1024 * 1024),
        )(*results)

    spec = P("view", "tok", None)
    return jax.shard_map(
        local, mesh=mesh, in_specs=(spec,) * 4, out_specs=(spec,) * 4, check_vma=False
    )
```

```python
import functools
import math

import jax
import jax.numpy as jnp
from jax import lax
from jax.experimental import pallas as pl
from jax.experimental.pallas import tpu as pltpu
from jax.sharding import PartitionSpec as P

HEADS = 16
PAD = 64
TILE = 16
NEG = -1e30
MESH = pl.DeviceIdType.MESH
F32 = jnp.float32
BF16 = jnp.bfloat16


def kernel(
    groups, parts, q_ref, k_ref, v_ref, g_ref, o_ref, dq_ref, dk_ref, dv_ref,
    qx, gx, kx, vx, in_from, in_to, out_from, out_to, tails, edge, got,
    kvp, kvt, ak, av,
    load_sem, in_send, in_recv, halo_send, halo_recv, part_send, part_recv, out_send, out_recv,
):
    views, toks, width = q_ref.shape
    lanes = kvp.shape[-1]
    half = lanes // 2
    share = width // parts
    chunks = share // lanes
    scale = 1.0 / math.sqrt(half)
    log2e = math.log2(math.e)
    whole8 = toks // 8 * 8
    up8 = (toks + 7) // 8 * 8
    bulk = toks // TILE * TILE
    rest = toks - bulk
    base = 2 * views * bulk
    tail_rows = in_from.shape[-2] - base
    me_v = lax.axis_index("view")
    me_t = lax.axis_index("tok")
    after = lax.rem(me_v + 1, groups)
    before = lax.rem(me_v + groups - 1, groups)
    peers = [lax.rem(me_t + s, parts) for s in range(parts)]

    ins = (q_ref, g_ref, k_ref, v_ref)
    loaded = (qx, gx, kx, vx)
    ROWS, PAIRS = 0, 1
    members = ((0, 1), (2, 3))

    def load(a, s):
        lanes_of = pl.ds(pl.multiple_of(peers[s] * share, lanes), share)
        return pltpu.make_async_copy(
            ins[a].at[:, :, lanes_of], loaded[a].at[s], load_sem.at[s, a]
        )

    for kind in (PAIRS, ROWS):
        for s in reversed(range(parts)):
            for a in members[kind]:
                load(a, s).start()

    barrier = pltpu.get_barrier_semaphore()
    for dev in [(before, me_t), (after, me_t)] + [(me_v, p) for p in peers[1:]]:
        pl.semaphore_signal(barrier, inc=1, device_id=dev, device_id_type=MESH)

    def span(owner, c):
        return pl.ds(pl.multiple_of(owner * share + c * lanes, lanes), lanes)

    def column(c):
        return pl.ds(pl.multiple_of(c * lanes, lanes), lanes)

    def in_copy(kind, c, s):
        return pltpu.make_async_remote_copy(
            src_ref=in_from.at[kind, c, s],
            dst_ref=in_to.at[kind, c, parts - s],
            send_sem=in_send.at[c, s, kind],
            recv_sem=in_recv.at[c, parts - s, kind],
            device_id=(me_v, peers[s]),
            device_id_type=MESH,
        )

    def halo_copy(c, way):
        src, dst, dev = ((1, views + 1, before), (views, 0, after))[way]
        return pltpu.make_async_remote_copy(
            src_ref=kvp.at[c, src],
            dst_ref=kvp.at[c, dst],
            send_sem=halo_send.at[c, way],
            recv_sem=halo_recv.at[c, way],
            device_id=(dev, me_t),
            device_id_type=MESH,
        )

    def part_copy(c, way):
        return pltpu.make_async_remote_copy(
            src_ref=edge.at[c, way],
            dst_ref=got.at[c, way],
            send_sem=part_send.at[c, way],
            recv_sem=part_recv.at[c, way],
            device_id=((before, after)[way], me_t),
            device_id_type=MESH,
        )

    outs = (o_ref, dq_ref, dk_ref, dv_ref)

    def out_copy(kind, c, s):
        return pltpu.make_async_remote_copy(
            src_ref=out_from.at[kind, c, s],
            dst_ref=out_to.at[kind, c, parts - s],
            send_sem=out_send.at[c, s, kind],
            recv_sem=out_recv.at[c, parts - s, kind],
            device_id=(me_v, peers[s]),
            device_id_type=MESH,
        )

    tail_row = lax.broadcasted_iota(jnp.int32, (tail_rows, lanes), 0)

    def send_in(kind, c):
        for s in range(1, parts):
            tail = jnp.zeros((tail_rows, lanes), F32)
            for i, a in enumerate(members[kind]):
                for v in range(views):
                    at = i * views + v
                    block = loaded[a][s, v, :, column(c)]
                    in_from[kind, c, s, at * bulk : (at + 1) * bulk] = block[:bulk]
                    for r in range(rest):
                        row = block[bulk + r : bulk + r + 1].astype(F32)
                        tail = jnp.where(tail_row == at * rest + r, row, tail)
            in_from[kind, c, s, base:] = tail.astype(BF16)
            in_copy(kind, c, s).start()

    for kind in (PAIRS, ROWS):
        for s in reversed(range(1, parts)):
            for a in members[kind]:
                load(a, s).wait()
        if kind == PAIRS:
            pl.semaphore_wait(barrier, parts + 1)
        send_in(kind, 0)
    if chunks > 1:
        send_in(PAIRS, 1)

    for a in range(4):
        load(a, 0).wait()

    pad_row = lax.broadcasted_iota(jnp.int32, (PAD - bulk, lanes), 0)

    def blocks_of(kind, i, c, s, v):
        if s == 0:
            block = loaded[members[kind][i]][0, v, :, column(c)]
            return jnp.concatenate([block, jnp.zeros((PAD - toks, lanes), BF16)], axis=0)
        at = i * views + v
        tail = in_to[kind, c, s, base:].astype(F32)
        end = jnp.zeros((PAD - bulk, lanes), F32)
        for r in range(rest):
            end = jnp.where(pad_row == r, tail[at * rest + r : at * rest + r + 1], end)
        main = in_to[kind, c, s, at * bulk : (at + 1) * bulk]
        return jnp.concatenate([main, end.astype(BF16)], axis=0)

    def relay(c):
        for s in range(1, parts):
            in_copy(PAIRS, c, parts - s).wait_recv()
        for v in range(views):
            for a in range(2):
                rows = [blocks_of(PAIRS, a, c, s, v) for s in range(parts)]
                kvp[c, v + 1, a] = jnp.concatenate(rows, axis=0)
        for way in range(2):
            halo_copy(c, way).start()
        for w in range(1, views + 1):
            turn(c, w)

    def turn(c, w):
        for a in range(2):
            kvt[c, w, a] = kvp[c, w, a].T

    def queries_ready(c):
        for s in range(1, parts):
            in_copy(ROWS, c, parts - s).wait_recv()

    def stage_halo(c):
        for way in range(2):
            halo_copy(c, way).wait_recv()
        turn(c, 0)
        turn(c, views + 1)

    def put(kind, i, c, s, v, block):
        at = i * views + v
        out_from[kind, c, s, at * bulk : (at + 1) * bulk] = block[:bulk].astype(BF16)
        for r in range(rest):
            row = at * rest + r
            tails[kind, s, row : row + 1] = block[bulk + r : bulk + r + 1]

    def send_out(kind, c):
        for s in range(1, parts):
            out_from[kind, c, s, base:] = tails[kind, s].astype(BF16)
            out_copy(kind, c, s).start()

    def take(kind, c, s):
        tail = out_to[kind, c, s, base:].astype(F32)
        for i, ref in enumerate(((o_ref, dq_ref), (dk_ref, dv_ref))[kind]):
            for v in range(views):
                at = i * views + v
                ref[v, :bulk, span(peers[s], c)] = out_to[kind, c, s, at * bulk : (at + 1) * bulk]
                if rest:
                    rows = tail[at * rest : (at + 1) * rest]
                    ref[v, bulk:toks, span(peers[s], c)] = rows.astype(BF16)

    lane = lax.broadcasted_iota(jnp.int32, (2 * PAD, lanes), 1)
    row_ok = lax.broadcasted_iota(jnp.int32, (up8 - whole8, 2 * lanes), 0) < toks - whole8
    blocks = 3 * parts

    def twin(x):
        zero = jnp.zeros_like(x)
        return jnp.concatenate([jnp.where(lane < half, x, zero), jnp.where(lane < half, zero, x)], 0)

    def full(x):
        filler = jnp.zeros((blocks, PAD - up8, 2 * lanes), F32)
        return jnp.concatenate([x, filler], axis=1).reshape(blocks * PAD, 2 * lanes).astype(BF16)

    def diagonal(x):
        return jnp.concatenate([x[:half, :lanes], x[half:, lanes:]], axis=0).T

    def dot(x, y):
        return jnp.dot(x, y, preferred_element_type=F32)

    def dot_t(x, y):
        return lax.dot_general(x, y, (((1,), (1,)), ((), ())), preferred_element_type=F32)

    def front(c, v, s):
        key_rows, value_rows = (
            jnp.concatenate([kvp[c, v + j, a] for j in range(3)], axis=0) for a in range(2)
        )
        query = jnp.concatenate([blocks_of(ROWS, 0, c, s + i, v) for i in range(2)], axis=0)
        grad = jnp.concatenate([blocks_of(ROWS, 1, c, s + i, v) for i in range(2)], axis=0)
        query = twin(query * jnp.asarray(scale, BF16))
        grad = twin(grad)
        scores = dot_t(key_rows, query).reshape(blocks, PAD, 2 * lanes)
        tail = jnp.where(row_ok[None], scores[:, whole8:up8], NEG)
        scores = jnp.concatenate([scores[:, :whole8], tail], axis=1)
        top = jnp.max(scores, axis=(0, 1), keepdims=True)
        probs = jnp.exp2((scores - top) * log2e)
        probs = probs * (1.0 / jnp.sum(probs, axis=(0, 1), keepdims=True))
        grad_probs = dot_t(value_rows, grad).reshape(blocks, PAD, 2 * lanes)[:, :up8]
        weighted = probs * grad_probs
        delta = jnp.sum(weighted, axis=(0, 1), keepdims=True)
        return query, grad, full(probs), full(weighted - probs * delta)

    def back(c, v, s, query, grad, probs_bf, grad_bf):
        now = lax.rem(c, 2)
        key_cols, value_cols = (
            jnp.concatenate([kvt[c, v + j, a] for j in range(3)], axis=1) for a in range(2)
        )
        ak[now, v : v + 3] += dot(grad_bf, query).reshape(3, parts * PAD, lanes)
        av[now, v : v + 3] += dot(probs_bf, grad).reshape(3, parts * PAD, lanes)
        attended = diagonal(dot(value_cols, probs_bf))
        query_grad = diagonal(dot(key_cols, grad_bf)) * scale
        for i in range(2):
            rows = slice(i * PAD, i * PAD + toks)
            if s + i == 0:
                o_ref[v, :, span(me_t, c)] = attended[rows].astype(BF16)
                dq_ref[v, :, span(me_t, c)] = query_grad[rows].astype(BF16)
            else:
                put(ROWS, 0, c, s + i, v, attended[rows])
                put(ROWS, 1, c, s + i, v, query_grad[rows])

    def compute(c, edge_views, inner_views):
        tasks = [(v, s) for v in edge_views + inner_views for s in range(0, parts, 2)]
        last_edge = len(edge_views) * (parts // 2)
        held = None
        for at, (v, s) in enumerate(tasks):
            made = front(c, v, s)
            if held is not None:
                back(c, *tasks[at - 1], *held)
                if at == last_edge:
                    send_parts(c)
            held = made
        if held is not None:
            back(c, *tasks[-1], *held)
        if len(tasks) == last_edge and last_edge:
            send_parts(c)

    def clear(c):
        now = lax.rem(c, 2)
        ak[now] = jnp.zeros(ak.shape[1:], F32)
        av[now] = jnp.zeros(av.shape[1:], F32)

    edge_views = [0, views - 1][: min(views, 2)]
    inner_views = list(range(1, views - 1))

    def send_parts(c):
        now = lax.rem(c, 2)
        for way, w in enumerate((0, views + 1)):
            for a, sums in enumerate((ak, av)):
                for s in range(parts):
                    edge[c, way, a, s] = sums[now, w, s * PAD : s * PAD + toks].astype(BF16)
            part_copy(c, way).start()

    def finish(c):
        now = lax.rem(c, 2)
        for way in range(2):
            part_copy(c, way).wait_recv()
        for s in reversed(range(parts)):
            for a, (sums, ref) in enumerate(((ak, dk_ref), (av, dv_ref))):
                for v in range(views):
                    total = sums[now, v + 1, s * PAD : s * PAD + toks]
                    if v == 0:
                        total = total + got[c, 1, a, s].astype(F32)
                    if v == views - 1:
                        total = total + got[c, 0, a, s].astype(F32)
                    if s == 0:
                        ref[v, :, span(me_t, c)] = total.astype(BF16)
                    else:
                        put(PAIRS, a, c, s, v, total)
            if s == 1:
                send_out(PAIRS, c)

    tails[...] = jnp.zeros_like(tails)
    relay(0)
    if chunks > 2:
        send_in(PAIRS, 2)
    clear(0)
    queries_ready(0)
    if chunks > 1:
        send_in(ROWS, 1)
    compute(0, [], inner_views)
    if chunks > 1:
        relay(1)
    if chunks > 3:
        send_in(PAIRS, 3)
    stage_halo(0)
    compute(0, edge_views, [])
    send_out(ROWS, 0)

    @pl.loop(1, chunks)
    def _(c):
        clear(c)

        @pl.when(c + 1 < chunks)
        def _():
            relay(c + 1)
            send_in(ROWS, c + 1)

        queries_ready(c)

        @pl.when(c + 3 < chunks)
        def _():
            send_in(PAIRS, c + 3)

        stage_halo(c)
        compute(c, edge_views, inner_views)
        send_out(ROWS, c)
        finish(c - 1)

    finish(chunks - 1)

    @pl.loop(0, chunks)
    def _(c):
        for kind in range(2):
            for s in range(1, parts):
                in_copy(kind, c, s).wait_send()
                out_copy(kind, c, s).wait_send()
                out_copy(kind, c, parts - s).wait_recv()
                take(kind, c, s)
        for way in range(2):
            part_copy(c, way).wait_send()
            halo_copy(c, way).wait_send()


def deliver(*refs):
    count = len(refs) // 2
    copies = [
        pltpu.make_async_copy(refs[i], refs[count + i], refs[-1].at[i]) for i in range(count)
    ]
    for copy in copies:
        copy.start()
    for copy in copies:
        copy.wait()


def solution(mesh):
    groups, parts = mesh.shape["view"], mesh.shape["tok"]

    def local(queries, keys, values, grad_out):
        views, toks, width = queries.shape
        lanes = 2 * (width // HEADS)
        chunks = width // parts // lanes
        vmem = pltpu.VMEM
        dma = pltpu.SemaphoreType.DMA
        bulk = toks // TILE * TILE
        tail = (2 * views * (toks - bulk) + 7) // 8 * 8
        source = vmem((parts, views, toks, width // parts), BF16)
        packed = vmem((2, chunks, parts, 2 * views * bulk + tail, lanes), BF16)
        edge = vmem((chunks, 2, 2, parts, toks, lanes), BF16)
        rows = vmem((chunks, views + 2, 2, parts * PAD, lanes), BF16)
        cols = vmem((chunks, views + 2, 2, lanes, parts * PAD), BF16)
        sums = vmem((2, views + 2, parts * PAD, lanes), F32)
        shape = jax.ShapeDtypeStruct(queries.shape, BF16)
        flops = 12 * views * parts * toks * 3 * parts * toks * (width // parts)
        results = pl.pallas_call(
            functools.partial(kernel, groups, parts),
            out_shape=(vmem(queries.shape, BF16),) * 4,
            in_specs=[pl.BlockSpec(memory_space=pl.ANY)] * 4,
            out_specs=[pl.BlockSpec(memory_space=pltpu.VMEM)] * 4,
            scratch_shapes=[
                source, source, source, source, packed, packed, packed, packed,
                vmem((2, parts, tail, lanes), F32), edge, edge, rows, cols, sums, sums,
                dma((parts, 4)), dma((chunks, parts, 2)), dma((chunks, parts, 2)),
                dma((chunks, 2)), dma((chunks, 2)), dma((chunks, 2)), dma((chunks, 2)),
                dma((chunks, parts, 2)), dma((chunks, parts, 2)),
            ],
            cost_estimate=pl.CostEstimate(
                flops=flops, bytes_accessed=16 * views * toks * width, transcendentals=0
            ),
            compiler_params=pltpu.CompilerParams(
                collective_id=0, has_side_effects=True, vmem_limit_bytes=58 * 1024 * 1024
            ),
        )(queries, keys, values, grad_out)
        return pl.pallas_call(
            deliver,
            out_shape=(shape,) * 4,
            in_specs=[pl.BlockSpec(memory_space=pltpu.VMEM)] * 4,
            out_specs=[pl.BlockSpec(memory_space=pl.ANY)] * 4,
            scratch_shapes=[dma((4,))],
            compiler_params=pltpu.CompilerParams(vmem_limit_bytes=48 * 1024 * 1024),
        )(*results)

    spec = P("view", "tok", None)
    return jax.shard_map(
        local, mesh=mesh, in_specs=(spec,) * 4, out_specs=(spec,) * 4, check_vma=False
    )
```

```python
import functools
import math

import jax
import jax.numpy as jnp
from jax import lax
from jax.experimental import pallas as pl
from jax.experimental.pallas import tpu as pltpu
from jax.sharding import PartitionSpec as P

HEADS = 16
PAD = 64
TILE = 16
NEG = -1e30
MESH = pl.DeviceIdType.MESH
F32 = jnp.float32
BF16 = jnp.bfloat16


def kernel(
    groups, parts, q_ref, k_ref, v_ref, g_ref, o_ref, dq_ref, dk_ref, dv_ref,
    qx, gx, kx, vx, in_from, in_to, out_from, out_to, tails, edge, got,
    kvp, kvt, ak, av,
    load_sem, in_send, in_recv, halo_send, halo_recv, part_send, part_recv, out_send, out_recv,
):
    views, toks, width = q_ref.shape
    lanes = kvp.shape[-1]
    half = lanes // 2
    share = width // parts
    chunks = share // lanes
    scale = 1.0 / math.sqrt(half)
    log2e = math.log2(math.e)
    whole8 = toks // 8 * 8
    up8 = (toks + 7) // 8 * 8
    bulk = toks // TILE * TILE
    rest = toks - bulk
    base = 2 * views * bulk
    tail_rows = in_from.shape[-2] - base
    me_v = lax.axis_index("view")
    me_t = lax.axis_index("tok")
    after = lax.rem(me_v + 1, groups)
    before = lax.rem(me_v + groups - 1, groups)
    peers = [lax.rem(me_t + s, parts) for s in range(parts)]

    ins = (q_ref, g_ref, k_ref, v_ref)
    loaded = (qx, gx, kx, vx)
    ROWS, PAIRS = 0, 1
    members = ((0, 1), (2, 3))

    def load(a, s):
        lanes_of = pl.ds(pl.multiple_of(peers[s] * share, lanes), share)
        return pltpu.make_async_copy(
            ins[a].at[:, :, lanes_of], loaded[a].at[s], load_sem.at[s, a]
        )

    for kind in (PAIRS, ROWS):
        for s in reversed(range(parts)):
            for a in members[kind]:
                load(a, s).start()

    barrier = pltpu.get_barrier_semaphore()
    for dev in [(before, me_t), (after, me_t)] + [(me_v, p) for p in peers[1:]]:
        pl.semaphore_signal(barrier, inc=1, device_id=dev, device_id_type=MESH)

    def span(owner, c):
        return pl.ds(pl.multiple_of(owner * share + c * lanes, lanes), lanes)

    def column(c):
        return pl.ds(pl.multiple_of(c * lanes, lanes), lanes)

    def in_copy(kind, c, s):
        return pltpu.make_async_remote_copy(
            src_ref=in_from.at[kind, c, s],
            dst_ref=in_to.at[kind, c, parts - s],
            send_sem=in_send.at[c, s, kind],
            recv_sem=in_recv.at[c, parts - s, kind],
            device_id=(me_v, peers[s]),
            device_id_type=MESH,
        )

    def halo_copy(c, way):
        src, dst, dev = ((1, views + 1, before), (views, 0, after))[way]
        return pltpu.make_async_remote_copy(
            src_ref=kvp.at[c, src],
            dst_ref=kvp.at[c, dst],
            send_sem=halo_send.at[c, way],
            recv_sem=halo_recv.at[c, way],
            device_id=(dev, me_t),
            device_id_type=MESH,
        )

    def part_copy(c, way):
        return pltpu.make_async_remote_copy(
            src_ref=edge.at[c, way],
            dst_ref=got.at[c, way],
            send_sem=part_send.at[c, way],
            recv_sem=part_recv.at[c, way],
            device_id=((before, after)[way], me_t),
            device_id_type=MESH,
        )

    outs = (o_ref, dq_ref, dk_ref, dv_ref)

    def out_copy(kind, c, s):
        return pltpu.make_async_remote_copy(
            src_ref=out_from.at[kind, c, s],
            dst_ref=out_to.at[kind, c, parts - s],
            send_sem=out_send.at[c, s, kind],
            recv_sem=out_recv.at[c, parts - s, kind],
            device_id=(me_v, peers[s]),
            device_id_type=MESH,
        )

    tail_row = lax.broadcasted_iota(jnp.int32, (tail_rows, lanes), 0)

    def send_in(kind, c):
        for s in range(1, parts):
            tail = jnp.zeros((tail_rows, lanes), F32)
            for i, a in enumerate(members[kind]):
                for v in range(views):
                    at = i * views + v
                    block = loaded[a][s, v, :, column(c)]
                    in_from[kind, c, s, at * bulk : (at + 1) * bulk] = block[:bulk]
                    for r in range(rest):
                        row = block[bulk + r : bulk + r + 1].astype(F32)
                        tail = jnp.where(tail_row == at * rest + r, row, tail)
            in_from[kind, c, s, base:] = tail.astype(BF16)
            in_copy(kind, c, s).start()

    for kind in (PAIRS, ROWS):
        for s in reversed(range(1, parts)):
            for a in members[kind]:
                load(a, s).wait()
        if kind == PAIRS:
            pl.semaphore_wait(barrier, parts + 1)
        send_in(kind, 0)
    if chunks > 1:
        send_in(PAIRS, 1)

    @pl.loop(1, chunks)
    def _(c):
        @pl.when(c + 1 < chunks)
        def _():
            send_in(PAIRS, c + 1)

        send_in(ROWS, c)

    for a in range(4):
        load(a, 0).wait()

    pad_row = lax.broadcasted_iota(jnp.int32, (PAD - bulk, lanes), 0)

    def blocks_of(kind, i, c, s, v):
        if s == 0:
            block = loaded[members[kind][i]][0, v, :, column(c)]
            return jnp.concatenate([block, jnp.zeros((PAD - toks, lanes), BF16)], axis=0)
        at = i * views + v
        tail = in_to[kind, c, s, base:].astype(F32)
        end = jnp.zeros((PAD - bulk, lanes), F32)
        for r in range(rest):
            end = jnp.where(pad_row == r, tail[at * rest + r : at * rest + r + 1], end)
        main = in_to[kind, c, s, at * bulk : (at + 1) * bulk]
        return jnp.concatenate([main, end.astype(BF16)], axis=0)

    def relay(c):
        for s in range(1, parts):
            in_copy(PAIRS, c, parts - s).wait_recv()
        for v in range(views):
            for a in range(2):
                rows = [blocks_of(PAIRS, a, c, s, v) for s in range(parts)]
                kvp[c, v + 1, a] = jnp.concatenate(rows, axis=0)
        for way in range(2):
            halo_copy(c, way).start()
        for w in range(1, views + 1):
            turn(c, w)

    def turn(c, w):
        for a in range(2):
            kvt[c, w, a] = kvp[c, w, a].T

    def queries_ready(c):
        for s in range(1, parts):
            in_copy(ROWS, c, parts - s).wait_recv()

    def stage_halo(c):
        for way in range(2):
            halo_copy(c, way).wait_recv()
        turn(c, 0)
        turn(c, views + 1)

    def put(kind, i, c, s, v, block):
        at = i * views + v
        out_from[kind, c, s, at * bulk : (at + 1) * bulk] = block[:bulk].astype(BF16)
        for r in range(rest):
            row = at * rest + r
            tails[kind, s, row : row + 1] = block[bulk + r : bulk + r + 1]

    def start_out(kind, c):
        for s in range(1, parts):
            out_copy(kind, c, s).start()

    def send_out(kind, c, step):
        for s in range(1, parts):
            out_from[kind, c, s, base:] = tails[kind, s].astype(BF16)

        @pl.when(step >= chunks - 2)
        def _():
            start_out(kind, c)

    def flush(step):
        @pl.when(step == chunks - 2)
        def _():
            @pl.loop(0, chunks - 2)
            def _(c):
                start_out(ROWS, c)

                @pl.when(c < chunks - 3)
                def _():
                    start_out(PAIRS, c)

    def take(kind, c, s):
        tail = out_to[kind, c, s, base:].astype(F32)
        for i, ref in enumerate(((o_ref, dq_ref), (dk_ref, dv_ref))[kind]):
            for v in range(views):
                at = i * views + v
                ref[v, :bulk, span(peers[s], c)] = out_to[kind, c, s, at * bulk : (at + 1) * bulk]
                if rest:
                    rows = tail[at * rest : (at + 1) * rest]
                    ref[v, bulk:toks, span(peers[s], c)] = rows.astype(BF16)

    lane = lax.broadcasted_iota(jnp.int32, (2 * PAD, lanes), 1)
    row_ok = lax.broadcasted_iota(jnp.int32, (up8 - whole8, 2 * lanes), 0) < toks - whole8
    blocks = 3 * parts

    def twin(x):
        zero = jnp.zeros_like(x)
        return jnp.concatenate([jnp.where(lane < half, x, zero), jnp.where(lane < half, zero, x)], 0)

    def full(x):
        filler = jnp.zeros((blocks, PAD - up8, 2 * lanes), F32)
        return jnp.concatenate([x, filler], axis=1).reshape(blocks * PAD, 2 * lanes).astype(BF16)

    def diagonal(x):
        return jnp.concatenate([x[:half, :lanes], x[half:, lanes:]], axis=0).T

    def dot(x, y):
        return jnp.dot(x, y, preferred_element_type=F32)

    def dot_t(x, y):
        return lax.dot_general(x, y, (((1,), (1,)), ((), ())), preferred_element_type=F32)

    def front(c, v, s):
        key_rows, value_rows = (
            jnp.concatenate([kvp[c, v + j, a] for j in range(3)], axis=0) for a in range(2)
        )
        query = jnp.concatenate([blocks_of(ROWS, 0, c, s + i, v) for i in range(2)], axis=0)
        grad = jnp.concatenate([blocks_of(ROWS, 1, c, s + i, v) for i in range(2)], axis=0)
        query = twin(query * jnp.asarray(scale, BF16))
        grad = twin(grad)
        scores = dot_t(key_rows, query).reshape(blocks, PAD, 2 * lanes)
        tail = jnp.where(row_ok[None], scores[:, whole8:up8], NEG)
        scores = jnp.concatenate([scores[:, :whole8], tail], axis=1)
        top = jnp.max(scores, axis=(0, 1), keepdims=True)
        probs = jnp.exp2((scores - top) * log2e)
        probs = probs * (1.0 / jnp.sum(probs, axis=(0, 1), keepdims=True))
        grad_probs = dot_t(value_rows, grad).reshape(blocks, PAD, 2 * lanes)[:, :up8]
        weighted = probs * grad_probs
        delta = jnp.sum(weighted, axis=(0, 1), keepdims=True)
        return query, grad, full(probs), full(weighted - probs * delta)

    def back(c, v, s, query, grad, probs_bf, grad_bf):
        now = lax.rem(c, 2)
        key_cols, value_cols = (
            jnp.concatenate([kvt[c, v + j, a] for j in range(3)], axis=1) for a in range(2)
        )
        ak[now, v : v + 3] += dot(grad_bf, query).reshape(3, parts * PAD, lanes)
        av[now, v : v + 3] += dot(probs_bf, grad).reshape(3, parts * PAD, lanes)
        attended = diagonal(dot(value_cols, probs_bf))
        query_grad = diagonal(dot(key_cols, grad_bf)) * scale
        for i in range(2):
            rows = slice(i * PAD, i * PAD + toks)
            if s + i == 0:
                o_ref[v, :, span(me_t, c)] = attended[rows].astype(BF16)
                dq_ref[v, :, span(me_t, c)] = query_grad[rows].astype(BF16)
            else:
                put(ROWS, 0, c, s + i, v, attended[rows])
                put(ROWS, 1, c, s + i, v, query_grad[rows])

    def compute(c, edge_views, inner_views, between=lambda: None):
        tasks = [(v, s) for v in edge_views + inner_views for s in range(0, parts, 2)]
        last_edge = len(edge_views) * (parts // 2)
        held = None
        for at, (v, s) in enumerate(tasks):
            made = front(c, v, s)
            if held is not None:
                back(c, *tasks[at - 1], *held)
                if at == last_edge:
                    send_parts(c)
                    between()
            held = made
        if held is not None:
            back(c, *tasks[-1], *held)
        if len(tasks) == last_edge and last_edge:
            send_parts(c)
            between()

    def clear(c):
        now = lax.rem(c, 2)
        ak[now] = jnp.zeros(ak.shape[1:], F32)
        av[now] = jnp.zeros(av.shape[1:], F32)

    edge_views = [0, views - 1][: min(views, 2)]
    inner_views = list(range(1, views - 1))

    def send_parts(c):
        now = lax.rem(c, 2)
        for way, w in enumerate((0, views + 1)):
            for a, sums in enumerate((ak, av)):
                for s in range(parts):
                    edge[c, way, a, s] = sums[now, w, s * PAD : s * PAD + toks].astype(BF16)
            part_copy(c, way).start()

    def finish(c, step):
        now = lax.rem(c, 2)
        for way in range(2):
            part_copy(c, way).wait_recv()
        for s in reversed(range(parts)):
            for a, (sums, ref) in enumerate(((ak, dk_ref), (av, dv_ref))):
                for v in range(views):
                    total = sums[now, v + 1, s * PAD : s * PAD + toks]
                    if v == 0:
                        total = total + got[c, 1, a, s].astype(F32)
                    if v == views - 1:
                        total = total + got[c, 0, a, s].astype(F32)
                    if s == 0:
                        ref[v, :, span(me_t, c)] = total.astype(BF16)
                    else:
                        put(PAIRS, a, c, s, v, total)
            if s == 1:
                send_out(PAIRS, c, step)

    tails[...] = jnp.zeros_like(tails)
    relay(0)
    clear(0)
    queries_ready(0)
    compute(0, [], inner_views)
    if chunks > 1:
        relay(1)
    stage_halo(0)
    compute(0, edge_views, [])
    send_out(ROWS, 0, 0)

    @pl.loop(1, chunks)
    def _(c):
        clear(c)

        @pl.when(c + 1 < chunks)
        def _():
            relay(c + 1)

        queries_ready(c)
        flush(c)
        stage_halo(c)
        compute(c, edge_views, inner_views, lambda: finish(c - 1, c))
        send_out(ROWS, c, c)

    finish(chunks - 1, chunks)

    @pl.loop(0, chunks)
    def _(c):
        for kind in range(2):
            for s in range(1, parts):
                in_copy(kind, c, s).wait_send()
                out_copy(kind, c, s).wait_send()
                out_copy(kind, c, parts - s).wait_recv()
                take(kind, c, s)
        for way in range(2):
            part_copy(c, way).wait_send()
            halo_copy(c, way).wait_send()


def deliver(*refs):
    count = len(refs) // 2
    copies = [
        pltpu.make_async_copy(refs[i], refs[count + i], refs[-1].at[i]) for i in range(count)
    ]
    for copy in copies:
        copy.start()
    for copy in copies:
        copy.wait()


def solution(mesh):
    groups, parts = mesh.shape["view"], mesh.shape["tok"]

    def local(queries, keys, values, grad_out):
        views, toks, width = queries.shape
        lanes = 2 * (width // HEADS)
        chunks = width // parts // lanes
        vmem = pltpu.VMEM
        dma = pltpu.SemaphoreType.DMA
        bulk = toks // TILE * TILE
        tail = (2 * views * (toks - bulk) + 7) // 8 * 8
        source = vmem((parts, views, toks, width // parts), BF16)
        packed = vmem((2, chunks, parts, 2 * views * bulk + tail, lanes), BF16)
        edge = vmem((chunks, 2, 2, parts, toks, lanes), BF16)
        rows = vmem((chunks, views + 2, 2, parts * PAD, lanes), BF16)
        cols = vmem((chunks, views + 2, 2, lanes, parts * PAD), BF16)
        sums = vmem((2, views + 2, parts * PAD, lanes), F32)
        shape = jax.ShapeDtypeStruct(queries.shape, BF16)
        flops = 12 * views * parts * toks * 3 * parts * toks * (width // parts)
        results = pl.pallas_call(
            functools.partial(kernel, groups, parts),
            out_shape=(vmem(queries.shape, BF16),) * 4,
            in_specs=[pl.BlockSpec(memory_space=pl.ANY)] * 4,
            out_specs=[pl.BlockSpec(memory_space=pltpu.VMEM)] * 4,
            scratch_shapes=[
                source, source, source, source, packed, packed, packed, packed,
                vmem((2, parts, tail, lanes), F32), edge, edge, rows, cols, sums, sums,
                dma((parts, 4)), dma((chunks, parts, 2)), dma((chunks, parts, 2)),
                dma((chunks, 2)), dma((chunks, 2)), dma((chunks, 2)), dma((chunks, 2)),
                dma((chunks, parts, 2)), dma((chunks, parts, 2)),
            ],
            cost_estimate=pl.CostEstimate(
                flops=flops, bytes_accessed=16 * views * toks * width, transcendentals=0
            ),
            compiler_params=pltpu.CompilerParams(
                collective_id=0, has_side_effects=True, vmem_limit_bytes=58 * 1024 * 1024
            ),
        )(queries, keys, values, grad_out)
        return pl.pallas_call(
            deliver,
            out_shape=(shape,) * 4,
            in_specs=[pl.BlockSpec(memory_space=pltpu.VMEM)] * 4,
            out_specs=[pl.BlockSpec(memory_space=pl.ANY)] * 4,
            scratch_shapes=[dma((4,))],
            compiler_params=pltpu.CompilerParams(vmem_limit_bytes=48 * 1024 * 1024),
        )(*results)

    spec = P("view", "tok", None)
    return jax.shard_map(
        local, mesh=mesh, in_specs=(spec,) * 4, out_specs=(spec,) * 4, check_vma=False
    )
```

```python
import functools
import math

import jax
import jax.numpy as jnp
from jax import lax
from jax.experimental import pallas as pl
from jax.experimental.pallas import tpu as pltpu
from jax.sharding import PartitionSpec as P

HEADS = 16
PAD = 64
TILE = 16
NEG = -1e30
MESH = pl.DeviceIdType.MESH
F32 = jnp.float32
BF16 = jnp.bfloat16


def kernel(
    groups, parts, q_ref, k_ref, v_ref, g_ref, o_ref, dq_ref, dk_ref, dv_ref,
    qx, gx, kx, vx, in_from, in_to, out_from, out_to, tails, edge, got,
    kvp, kvt, ak, av,
    load_sem, in_send, in_recv, halo_send, halo_recv, part_send, part_recv, out_send, out_recv,
):
    views, toks, width = q_ref.shape
    lanes = kvp.shape[-1]
    half = lanes // 2
    share = width // parts
    chunks = share // lanes
    scale = 1.0 / math.sqrt(half)
    log2e = math.log2(math.e)
    whole8 = toks // 8 * 8
    up8 = (toks + 7) // 8 * 8
    bulk = toks // TILE * TILE
    rest = toks - bulk
    base = 2 * views * bulk
    tail_rows = in_from.shape[-2] - base
    me_v = lax.axis_index("view")
    me_t = lax.axis_index("tok")
    after = lax.rem(me_v + 1, groups)
    before = lax.rem(me_v + groups - 1, groups)
    peers = [lax.rem(me_t + s, parts) for s in range(parts)]

    ins = (q_ref, g_ref, k_ref, v_ref)
    loaded = (qx, gx, kx, vx)
    ROWS, PAIRS = 0, 1
    members = ((0, 1), (2, 3))

    def load(a, s):
        lanes_of = pl.ds(pl.multiple_of(peers[s] * share, lanes), share)
        return pltpu.make_async_copy(
            ins[a].at[:, :, lanes_of], loaded[a].at[s], load_sem.at[s, a]
        )

    for kind in (PAIRS, ROWS):
        for s in reversed(range(parts)):
            for a in members[kind]:
                load(a, s).start()

    barrier = pltpu.get_barrier_semaphore()
    for dev in [(before, me_t), (after, me_t)] + [(me_v, p) for p in peers[1:]]:
        pl.semaphore_signal(barrier, inc=1, device_id=dev, device_id_type=MESH)

    def span(owner, c):
        return pl.ds(pl.multiple_of(owner * share + c * lanes, lanes), lanes)

    def column(c):
        return pl.ds(pl.multiple_of(c * lanes, lanes), lanes)

    def in_copy(kind, c, s):
        return pltpu.make_async_remote_copy(
            src_ref=in_from.at[kind, c, s],
            dst_ref=in_to.at[kind, c, parts - s],
            send_sem=in_send.at[c, s, kind],
            recv_sem=in_recv.at[c, parts - s, kind],
            device_id=(me_v, peers[s]),
            device_id_type=MESH,
        )

    def halo_copy(c, way):
        src, dst, dev = ((1, views + 1, before), (views, 0, after))[way]
        return pltpu.make_async_remote_copy(
            src_ref=kvp.at[c, src],
            dst_ref=kvp.at[c, dst],
            send_sem=halo_send.at[c, way],
            recv_sem=halo_recv.at[c, way],
            device_id=(dev, me_t),
            device_id_type=MESH,
        )

    def part_copy(c, way):
        return pltpu.make_async_remote_copy(
            src_ref=edge.at[c, way],
            dst_ref=got.at[c, way],
            send_sem=part_send.at[c, way],
            recv_sem=part_recv.at[c, way],
            device_id=((before, after)[way], me_t),
            device_id_type=MESH,
        )

    outs = (o_ref, dq_ref, dk_ref, dv_ref)

    def out_copy(kind, c, s):
        return pltpu.make_async_remote_copy(
            src_ref=out_from.at[kind, c, s],
            dst_ref=out_to.at[kind, c, parts - s],
            send_sem=out_send.at[c, s, kind],
            recv_sem=out_recv.at[c, parts - s, kind],
            device_id=(me_v, peers[s]),
            device_id_type=MESH,
        )

    tail_row = lax.broadcasted_iota(jnp.int32, (tail_rows, lanes), 0)

    def send_in(kind, c):
        for s in range(1, parts):
            tail = jnp.zeros((tail_rows, lanes), F32)
            for i, a in enumerate(members[kind]):
                for v in range(views):
                    at = i * views + v
                    block = loaded[a][s, v, :, column(c)]
                    in_from[kind, c, s, at * bulk : (at + 1) * bulk] = block[:bulk]
                    for r in range(rest):
                        row = block[bulk + r : bulk + r + 1].astype(F32)
                        tail = jnp.where(tail_row == at * rest + r, row, tail)
            in_from[kind, c, s, base:] = tail.astype(BF16)
            in_copy(kind, c, s).start()

    for kind in (PAIRS, ROWS):
        for s in reversed(range(1, parts)):
            for a in members[kind]:
                load(a, s).wait()
        if kind == PAIRS:
            pl.semaphore_wait(barrier, parts + 1)
        send_in(kind, 0)
    if chunks > 1:
        send_in(PAIRS, 1)

    @pl.loop(1, chunks)
    def _(c):
        @pl.when(c + 1 < chunks)
        def _():
            send_in(PAIRS, c + 1)

        send_in(ROWS, c)

    for a in range(4):
        load(a, 0).wait()

    pad_row = lax.broadcasted_iota(jnp.int32, (PAD - bulk, lanes), 0)

    def blocks_of(kind, i, c, s, v):
        if s == 0:
            block = loaded[members[kind][i]][0, v, :, column(c)]
            return jnp.concatenate([block, jnp.zeros((PAD - toks, lanes), BF16)], axis=0)
        at = i * views + v
        tail = in_to[kind, c, s, base:].astype(F32)
        end = jnp.zeros((PAD - bulk, lanes), F32)
        for r in range(rest):
            end = jnp.where(pad_row == r, tail[at * rest + r : at * rest + r + 1], end)
        main = in_to[kind, c, s, at * bulk : (at + 1) * bulk]
        return jnp.concatenate([main, end.astype(BF16)], axis=0)

    def relay(c):
        for s in range(1, parts):
            in_copy(PAIRS, c, parts - s).wait_recv()
        for v in range(views):
            for a in range(2):
                rows = [blocks_of(PAIRS, a, c, s, v) for s in range(parts)]
                kvp[c, v + 1, a] = jnp.concatenate(rows, axis=0)
        for way in range(2):
            halo_copy(c, way).start()
        for w in range(1, views + 1):
            turn(c, w)

    def turn(c, w):
        for a in range(2):
            kvt[c, w, a] = kvp[c, w, a].T

    def queries_ready(c):
        for s in range(1, parts):
            in_copy(ROWS, c, parts - s).wait_recv()

    def stage_halo(c):
        for way in range(2):
            halo_copy(c, way).wait_recv()
        turn(c, 0)
        turn(c, views + 1)

    def put(kind, i, c, s, v, block):
        at = i * views + v
        out_from[kind, c, s, at * bulk : (at + 1) * bulk] = block[:bulk].astype(BF16)
        for r in range(rest):
            row = at * rest + r
            tails[kind, s, row : row + 1] = block[bulk + r : bulk + r + 1]

    def send_out(kind, c):
        for s in range(1, parts):
            out_from[kind, c, s, base:] = tails[kind, s].astype(BF16)
            out_copy(kind, c, s).start()

    def take(kind, c, s):
        tail = out_to[kind, c, s, base:].astype(F32)
        for i, ref in enumerate(((o_ref, dq_ref), (dk_ref, dv_ref))[kind]):
            for v in range(views):
                at = i * views + v
                ref[v, :bulk, span(peers[s], c)] = out_to[kind, c, s, at * bulk : (at + 1) * bulk]
                if rest:
                    rows = tail[at * rest : (at + 1) * rest]
                    ref[v, bulk:toks, span(peers[s], c)] = rows.astype(BF16)

    lane = lax.broadcasted_iota(jnp.int32, (2 * PAD, lanes), 1)
    row_ok = lax.broadcasted_iota(jnp.int32, (up8 - whole8, 2 * lanes), 0) < toks - whole8
    blocks = 3 * parts

    def twin(x):
        zero = jnp.zeros_like(x)
        return jnp.concatenate([jnp.where(lane < half, x, zero), jnp.where(lane < half, zero, x)], 0)

    def full(x):
        filler = jnp.zeros((blocks, PAD - up8, 2 * lanes), F32)
        return jnp.concatenate([x, filler], axis=1).reshape(blocks * PAD, 2 * lanes).astype(BF16)

    def diagonal(x):
        return jnp.concatenate([x[:half, :lanes], x[half:, lanes:]], axis=0).T

    def dot(x, y):
        return jnp.dot(x, y, preferred_element_type=F32)

    def dot_t(x, y):
        return lax.dot_general(x, y, (((1,), (1,)), ((), ())), preferred_element_type=F32)

    def front(c, v, s):
        key_rows, value_rows = (
            jnp.concatenate([kvp[c, v + j, a] for j in range(3)], axis=0) for a in range(2)
        )
        query = jnp.concatenate([blocks_of(ROWS, 0, c, s + i, v) for i in range(2)], axis=0)
        grad = jnp.concatenate([blocks_of(ROWS, 1, c, s + i, v) for i in range(2)], axis=0)
        query = twin(query * jnp.asarray(scale, BF16))
        grad = twin(grad)
        scores = dot_t(key_rows, query).reshape(blocks, PAD, 2 * lanes)
        tail = jnp.where(row_ok[None], scores[:, whole8:up8], NEG)
        scores = jnp.concatenate([scores[:, :whole8], tail], axis=1)
        top = jnp.max(scores, axis=(0, 1), keepdims=True)
        probs = jnp.exp2((scores - top) * log2e)
        probs = probs * (1.0 / jnp.sum(probs, axis=(0, 1), keepdims=True))
        grad_probs = dot_t(value_rows, grad).reshape(blocks, PAD, 2 * lanes)[:, :up8]
        weighted = probs * grad_probs
        delta = jnp.sum(weighted, axis=(0, 1), keepdims=True)
        return query, grad, full(probs), full(weighted - probs * delta)

    def back(c, v, s, query, grad, probs_bf, grad_bf):
        now = lax.rem(c, 2)
        key_cols, value_cols = (
            jnp.concatenate([kvt[c, v + j, a] for j in range(3)], axis=1) for a in range(2)
        )
        ak[now, v : v + 3] += dot(grad_bf, query).reshape(3, parts * PAD, lanes)
        av[now, v : v + 3] += dot(probs_bf, grad).reshape(3, parts * PAD, lanes)
        attended = diagonal(dot(value_cols, probs_bf))
        query_grad = diagonal(dot(key_cols, grad_bf)) * scale
        for i in range(2):
            rows = slice(i * PAD, i * PAD + toks)
            if s + i == 0:
                o_ref[v, :, span(me_t, c)] = attended[rows].astype(BF16)
                dq_ref[v, :, span(me_t, c)] = query_grad[rows].astype(BF16)
            else:
                put(ROWS, 0, c, s + i, v, attended[rows])
                put(ROWS, 1, c, s + i, v, query_grad[rows])

    def compute(c, edge_views, inner_views, between=lambda: None):
        tasks = [(v, s) for v in edge_views + inner_views for s in range(0, parts, 2)]
        last_edge = len(edge_views) * (parts // 2)
        held = None
        for at, (v, s) in enumerate(tasks):
            made = front(c, v, s)
            if held is not None:
                back(c, *tasks[at - 1], *held)
                if at == last_edge:
                    send_parts(c)
                    between()
            held = made
        if held is not None:
            back(c, *tasks[-1], *held)
        if len(tasks) == last_edge and last_edge:
            send_parts(c)
            between()

    def clear(c):
        now = lax.rem(c, 2)
        ak[now] = jnp.zeros(ak.shape[1:], F32)
        av[now] = jnp.zeros(av.shape[1:], F32)

    edge_views = [0, views - 1][: min(views, 2)]
    inner_views = list(range(1, views - 1))

    def send_parts(c):
        now = lax.rem(c, 2)
        for way, w in enumerate((0, views + 1)):
            for a, sums in enumerate((ak, av)):
                for s in range(parts):
                    edge[c, way, a, s] = sums[now, w, s * PAD : s * PAD + toks].astype(BF16)
            part_copy(c, way).start()

    def finish(c):
        now = lax.rem(c, 2)
        for way in range(2):
            part_copy(c, way).wait_recv()
        for s in reversed(range(parts)):
            for a, (sums, ref) in enumerate(((ak, dk_ref), (av, dv_ref))):
                for v in range(views):
                    total = sums[now, v + 1, s * PAD : s * PAD + toks]
                    if v == 0:
                        total = total + got[c, 1, a, s].astype(F32)
                    if v == views - 1:
                        total = total + got[c, 0, a, s].astype(F32)
                    if s == 0:
                        ref[v, :, span(me_t, c)] = total.astype(BF16)
                    else:
                        put(PAIRS, a, c, s, v, total)
            if s == 1:
                send_out(PAIRS, c)

    tails[...] = jnp.zeros_like(tails)
    relay(0)
    clear(0)
    queries_ready(0)
    compute(0, [], inner_views)
    if chunks > 1:
        relay(1)
    stage_halo(0)
    compute(0, edge_views, [])
    send_out(ROWS, 0)

    @pl.loop(1, chunks)
    def _(c):
        clear(c)

        @pl.when(c + 1 < chunks)
        def _():
            relay(c + 1)

        queries_ready(c)
        stage_halo(c)
        compute(c, edge_views, inner_views, lambda: finish(c - 1))
        send_out(ROWS, c)

    finish(chunks - 1)

    @pl.loop(0, chunks)
    def _(c):
        for kind in range(2):
            for s in range(1, parts):
                in_copy(kind, c, s).wait_send()
                out_copy(kind, c, s).wait_send()
                out_copy(kind, c, parts - s).wait_recv()
                take(kind, c, s)
        for way in range(2):
            part_copy(c, way).wait_send()
            halo_copy(c, way).wait_send()


def deliver(*refs):
    count = len(refs) // 2
    copies = [
        pltpu.make_async_copy(refs[i], refs[count + i], refs[-1].at[i]) for i in range(count)
    ]
    for copy in copies:
        copy.start()
    for copy in copies:
        copy.wait()


def solution(mesh):
    groups, parts = mesh.shape["view"], mesh.shape["tok"]

    def local(queries, keys, values, grad_out):
        views, toks, width = queries.shape
        lanes = 2 * (width // HEADS)
        chunks = width // parts // lanes
        vmem = pltpu.VMEM
        dma = pltpu.SemaphoreType.DMA
        bulk = toks // TILE * TILE
        tail = (2 * views * (toks - bulk) + 7) // 8 * 8
        source = vmem((parts, views, toks, width // parts), BF16)
        packed = vmem((2, chunks, parts, 2 * views * bulk + tail, lanes), BF16)
        edge = vmem((chunks, 2, 2, parts, toks, lanes), BF16)
        rows = vmem((chunks, views + 2, 2, parts * PAD, lanes), BF16)
        cols = vmem((chunks, views + 2, 2, lanes, parts * PAD), BF16)
        sums = vmem((2, views + 2, parts * PAD, lanes), F32)
        shape = jax.ShapeDtypeStruct(queries.shape, BF16)
        flops = 12 * views * parts * toks * 3 * parts * toks * (width // parts)
        results = pl.pallas_call(
            functools.partial(kernel, groups, parts),
            out_shape=(vmem(queries.shape, BF16),) * 4,
            in_specs=[pl.BlockSpec(memory_space=pl.ANY)] * 4,
            out_specs=[pl.BlockSpec(memory_space=pltpu.VMEM)] * 4,
            scratch_shapes=[
                source, source, source, source, packed, packed, packed, packed,
                vmem((2, parts, tail, lanes), F32), edge, edge, rows, cols, sums, sums,
                dma((parts, 4)), dma((chunks, parts, 2)), dma((chunks, parts, 2)),
                dma((chunks, 2)), dma((chunks, 2)), dma((chunks, 2)), dma((chunks, 2)),
                dma((chunks, parts, 2)), dma((chunks, parts, 2)),
            ],
            cost_estimate=pl.CostEstimate(
                flops=flops, bytes_accessed=16 * views * toks * width, transcendentals=0
            ),
            compiler_params=pltpu.CompilerParams(
                collective_id=0, has_side_effects=True, vmem_limit_bytes=58 * 1024 * 1024
            ),
        )(queries, keys, values, grad_out)
        return pl.pallas_call(
            deliver,
            out_shape=(shape,) * 4,
            in_specs=[pl.BlockSpec(memory_space=pltpu.VMEM)] * 4,
            out_specs=[pl.BlockSpec(memory_space=pl.ANY)] * 4,
            scratch_shapes=[dma((4,))],
            compiler_params=pltpu.CompilerParams(vmem_limit_bytes=48 * 1024 * 1024),
        )(*results)

    spec = P("view", "tok", None)
    return jax.shard_map(
        local, mesh=mesh, in_specs=(spec,) * 4, out_specs=(spec,) * 4, check_vma=False
    )
```

```python
import functools
import math

import jax
import jax.numpy as jnp
from jax import lax
from jax.experimental import pallas as pl
from jax.experimental.pallas import tpu as pltpu
from jax.sharding import PartitionSpec as P

HEADS = 16
PAD = 64
TILE = 16
NEG = -1e30
MESH = pl.DeviceIdType.MESH
F32 = jnp.float32
BF16 = jnp.bfloat16


def kernel(
    groups, parts, q_ref, k_ref, v_ref, g_ref, o_ref, dq_ref, dk_ref, dv_ref,
    qx, gx, kx, vx, in_from, in_to, out_from, out_to, tails, edge, got,
    kvp, kvt, ak, av,
    load_sem, in_send, in_recv, halo_send, halo_recv, part_send, part_recv, out_send, out_recv,
):
    views, toks, width = q_ref.shape
    lanes = kvp.shape[-1]
    half = lanes // 2
    share = width // parts
    chunks = share // lanes
    scale = 1.0 / math.sqrt(half)
    log2e = math.log2(math.e)
    whole8 = toks // 8 * 8
    up8 = (toks + 7) // 8 * 8
    bulk = toks // TILE * TILE
    rest = toks - bulk
    base = 2 * views * bulk
    tail_rows = in_from.shape[-2] - base
    me_v = lax.axis_index("view")
    me_t = lax.axis_index("tok")
    after = lax.rem(me_v + 1, groups)
    before = lax.rem(me_v + groups - 1, groups)
    peers = [lax.rem(me_t + s, parts) for s in range(parts)]

    ins = (q_ref, g_ref, k_ref, v_ref)
    loaded = (qx, gx, kx, vx)
    ROWS, PAIRS = 0, 1
    members = ((0, 1), (2, 3))

    def load(a, s):
        lanes_of = pl.ds(pl.multiple_of(peers[s] * share, lanes), share)
        return pltpu.make_async_copy(
            ins[a].at[:, :, lanes_of], loaded[a].at[s], load_sem.at[s, a]
        )

    for kind in (PAIRS, ROWS):
        for s in reversed(range(parts)):
            for a in members[kind]:
                load(a, s).start()

    barrier = pltpu.get_barrier_semaphore()
    for dev in [(before, me_t), (after, me_t)] + [(me_v, p) for p in peers[1:]]:
        pl.semaphore_signal(barrier, inc=1, device_id=dev, device_id_type=MESH)

    def span(owner, c):
        return pl.ds(pl.multiple_of(owner * share + c * lanes, lanes), lanes)

    def column(c):
        return pl.ds(pl.multiple_of(c * lanes, lanes), lanes)

    def in_copy(kind, c, s):
        return pltpu.make_async_remote_copy(
            src_ref=in_from.at[kind, c, s],
            dst_ref=in_to.at[kind, c, parts - s],
            send_sem=in_send.at[c, s, kind],
            recv_sem=in_recv.at[c, parts - s, kind],
            device_id=(me_v, peers[s]),
            device_id_type=MESH,
        )

    def halo_copy(c, way):
        src, dst, dev = ((1, views + 1, before), (views, 0, after))[way]
        return pltpu.make_async_remote_copy(
            src_ref=kvp.at[c, src],
            dst_ref=kvp.at[c, dst],
            send_sem=halo_send.at[c, way],
            recv_sem=halo_recv.at[c, way],
            device_id=(dev, me_t),
            device_id_type=MESH,
        )

    def part_copy(c, way):
        return pltpu.make_async_remote_copy(
            src_ref=edge.at[c, way],
            dst_ref=got.at[c, way],
            send_sem=part_send.at[c, way],
            recv_sem=part_recv.at[c, way],
            device_id=((before, after)[way], me_t),
            device_id_type=MESH,
        )

    outs = (o_ref, dq_ref, dk_ref, dv_ref)

    def out_copy(kind, c, s):
        return pltpu.make_async_remote_copy(
            src_ref=out_from.at[kind, c, s],
            dst_ref=out_to.at[kind, c, parts - s],
            send_sem=out_send.at[c, s, kind],
            recv_sem=out_recv.at[c, parts - s, kind],
            device_id=(me_v, peers[s]),
            device_id_type=MESH,
        )

    tail_row = lax.broadcasted_iota(jnp.int32, (tail_rows, lanes), 0)

    def send_in(kind, c):
        for s in range(1, parts):
            tail = jnp.zeros((tail_rows, lanes), F32)
            for i, a in enumerate(members[kind]):
                for v in range(views):
                    at = i * views + v
                    block = loaded[a][s, v, :, column(c)]
                    in_from[kind, c, s, at * bulk : (at + 1) * bulk] = block[:bulk]
                    for r in range(rest):
                        row = block[bulk + r : bulk + r + 1].astype(F32)
                        tail = jnp.where(tail_row == at * rest + r, row, tail)
            in_from[kind, c, s, base:] = tail.astype(BF16)
            in_copy(kind, c, s).start()

    for kind in (PAIRS, ROWS):
        for s in reversed(range(1, parts)):
            for a in members[kind]:
                load(a, s).wait()
        if kind == PAIRS:
            pl.semaphore_wait(barrier, parts + 1)
        send_in(kind, 0)

    @pl.loop(1, chunks)
    def _(c):
        send_in(PAIRS, c)
        send_in(ROWS, c)

    for a in range(4):
        load(a, 0).wait()

    pad_row = lax.broadcasted_iota(jnp.int32, (PAD - bulk, lanes), 0)

    def blocks_of(kind, i, c, s, v):
        if s == 0:
            block = loaded[members[kind][i]][0, v, :, column(c)]
            return jnp.concatenate([block, jnp.zeros((PAD - toks, lanes), BF16)], axis=0)
        at = i * views + v
        tail = in_to[kind, c, s, base:].astype(F32)
        end = jnp.zeros((PAD - bulk, lanes), F32)
        for r in range(rest):
            end = jnp.where(pad_row == r, tail[at * rest + r : at * rest + r + 1], end)
        main = in_to[kind, c, s, at * bulk : (at + 1) * bulk]
        return jnp.concatenate([main, end.astype(BF16)], axis=0)

    def relay(c):
        for s in range(1, parts):
            in_copy(PAIRS, c, parts - s).wait_recv()
        for v in range(views):
            for a in range(2):
                rows = [blocks_of(PAIRS, a, c, s, v) for s in range(parts)]
                kvp[c, v + 1, a] = jnp.concatenate(rows, axis=0)
        for way in range(2):
            halo_copy(c, way).start()
        for w in range(1, views + 1):
            turn(c, w)

    def turn(c, w):
        for a in range(2):
            kvt[c, w, a] = kvp[c, w, a].T

    def queries_ready(c):
        for s in range(1, parts):
            in_copy(ROWS, c, parts - s).wait_recv()

    def stage_halo(c):
        for way in range(2):
            halo_copy(c, way).wait_recv()
        turn(c, 0)
        turn(c, views + 1)

    def put(kind, i, c, s, v, block):
        at = i * views + v
        out_from[kind, c, s, at * bulk : (at + 1) * bulk] = block[:bulk].astype(BF16)
        for r in range(rest):
            row = at * rest + r
            tails[kind, s, row : row + 1] = block[bulk + r : bulk + r + 1]

    def send_out(kind, c):
        for s in range(1, parts):
            out_from[kind, c, s, base:] = tails[kind, s].astype(BF16)
            out_copy(kind, c, s).start()

    def take(kind, c, s):
        tail = out_to[kind, c, s, base:].astype(F32)
        for i, ref in enumerate(((o_ref, dq_ref), (dk_ref, dv_ref))[kind]):
            for v in range(views):
                at = i * views + v
                ref[v, :bulk, span(peers[s], c)] = out_to[kind, c, s, at * bulk : (at + 1) * bulk]
                if rest:
                    rows = tail[at * rest : (at + 1) * rest]
                    ref[v, bulk:toks, span(peers[s], c)] = rows.astype(BF16)

    lane = lax.broadcasted_iota(jnp.int32, (2 * PAD, lanes), 1)
    row_ok = lax.broadcasted_iota(jnp.int32, (up8 - whole8, 2 * lanes), 0) < toks - whole8
    blocks = 3 * parts

    def twin(x):
        zero = jnp.zeros_like(x)
        return jnp.concatenate([jnp.where(lane < half, x, zero), jnp.where(lane < half, zero, x)], 0)

    def full(x):
        filler = jnp.zeros((blocks, PAD - up8, 2 * lanes), F32)
        return jnp.concatenate([x, filler], axis=1).reshape(blocks * PAD, 2 * lanes).astype(BF16)

    def diagonal(x):
        return jnp.concatenate([x[:half, :lanes], x[half:, lanes:]], axis=0).T

    def dot(x, y):
        return jnp.dot(x, y, preferred_element_type=F32)

    def dot_t(x, y):
        return lax.dot_general(x, y, (((1,), (1,)), ((), ())), preferred_element_type=F32)

    def front(c, v, s):
        key_rows, value_rows = (
            jnp.concatenate([kvp[c, v + j, a] for j in range(3)], axis=0) for a in range(2)
        )
        query = jnp.concatenate([blocks_of(ROWS, 0, c, s + i, v) for i in range(2)], axis=0)
        grad = jnp.concatenate([blocks_of(ROWS, 1, c, s + i, v) for i in range(2)], axis=0)
        query = twin(query * jnp.asarray(scale, BF16))
        grad = twin(grad)
        scores = dot_t(key_rows, query).reshape(blocks, PAD, 2 * lanes)
        tail = jnp.where(row_ok[None], scores[:, whole8:up8], NEG)
        scores = jnp.concatenate([scores[:, :whole8], tail], axis=1)
        top = jnp.max(scores, axis=(0, 1), keepdims=True)
        probs = jnp.exp2((scores - top) * log2e)
        probs = probs * (1.0 / jnp.sum(probs, axis=(0, 1), keepdims=True))
        grad_probs = dot_t(value_rows, grad).reshape(blocks, PAD, 2 * lanes)[:, :up8]
        weighted = probs * grad_probs
        delta = jnp.sum(weighted, axis=(0, 1), keepdims=True)
        return query, grad, full(probs), full(weighted - probs * delta)

    def back(c, v, s, query, grad, probs_bf, grad_bf):
        now = lax.rem(c, 2)
        key_cols, value_cols = (
            jnp.concatenate([kvt[c, v + j, a] for j in range(3)], axis=1) for a in range(2)
        )
        ak[now, v : v + 3] += dot(grad_bf, query).reshape(3, parts * PAD, lanes)
        av[now, v : v + 3] += dot(probs_bf, grad).reshape(3, parts * PAD, lanes)
        attended = diagonal(dot(value_cols, probs_bf))
        query_grad = diagonal(dot(key_cols, grad_bf)) * scale
        for i in range(2):
            rows = slice(i * PAD, i * PAD + toks)
            if s + i == 0:
                o_ref[v, :, span(me_t, c)] = attended[rows].astype(BF16)
                dq_ref[v, :, span(me_t, c)] = query_grad[rows].astype(BF16)
            else:
                put(ROWS, 0, c, s + i, v, attended[rows])
                put(ROWS, 1, c, s + i, v, query_grad[rows])

    def compute(c, edge_views, inner_views, between=lambda: None):
        tasks = [(v, s) for v in edge_views + inner_views for s in range(0, parts, 2)]
        last_edge = len(edge_views) * (parts // 2)
        held = None
        for at, (v, s) in enumerate(tasks):
            made = front(c, v, s)
            if held is not None:
                back(c, *tasks[at - 1], *held)
                if at == last_edge:
                    send_parts(c)
                    between()
            held = made
        if held is not None:
            back(c, *tasks[-1], *held)
        if len(tasks) == last_edge and last_edge:
            send_parts(c)
            between()

    def clear(c):
        now = lax.rem(c, 2)
        ak[now] = jnp.zeros(ak.shape[1:], F32)
        av[now] = jnp.zeros(av.shape[1:], F32)

    edge_views = [0, views - 1][: min(views, 2)]
    inner_views = list(range(1, views - 1))

    def send_parts(c):
        now = lax.rem(c, 2)
        for way, w in enumerate((0, views + 1)):
            for a, sums in enumerate((ak, av)):
                for s in range(parts):
                    edge[c, way, a, s] = sums[now, w, s * PAD : s * PAD + toks].astype(BF16)
            part_copy(c, way).start()

    def finish(c):
        now = lax.rem(c, 2)
        for way in range(2):
            part_copy(c, way).wait_recv()
        for s in reversed(range(parts)):
            for a, (sums, ref) in enumerate(((ak, dk_ref), (av, dv_ref))):
                for v in range(views):
                    total = sums[now, v + 1, s * PAD : s * PAD + toks]
                    if v == 0:
                        total = total + got[c, 1, a, s].astype(F32)
                    if v == views - 1:
                        total = total + got[c, 0, a, s].astype(F32)
                    if s == 0:
                        ref[v, :, span(me_t, c)] = total.astype(BF16)
                    else:
                        put(PAIRS, a, c, s, v, total)
            if s == 1:
                send_out(PAIRS, c)

    tails[...] = jnp.zeros_like(tails)
    def advance(c):
        @pl.when(c + 1 < chunks)
        def _():
            relay(c + 1)

        finish(c - 1)

    relay(0)
    clear(0)
    queries_ready(0)
    compute(0, [], inner_views)
    if chunks > 1:
        relay(1)
    stage_halo(0)
    compute(0, edge_views, [])
    send_out(ROWS, 0)

    @pl.loop(1, chunks)
    def _(c):
        clear(c)

        queries_ready(c)
        stage_halo(c)
        compute(c, edge_views, inner_views, lambda: advance(c))
        send_out(ROWS, c)

    finish(chunks - 1)

    @pl.loop(0, chunks)
    def _(c):
        for kind in range(2):
            for s in range(1, parts):
                in_copy(kind, c, s).wait_send()
                out_copy(kind, c, s).wait_send()
                out_copy(kind, c, parts - s).wait_recv()
                take(kind, c, s)
        for way in range(2):
            part_copy(c, way).wait_send()
            halo_copy(c, way).wait_send()


def deliver(*refs):
    count = len(refs) // 2
    copies = [
        pltpu.make_async_copy(refs[i], refs[count + i], refs[-1].at[i]) for i in range(count)
    ]
    for copy in copies:
        copy.start()
    for copy in copies:
        copy.wait()


def solution(mesh):
    groups, parts = mesh.shape["view"], mesh.shape["tok"]

    def local(queries, keys, values, grad_out):
        views, toks, width = queries.shape
        lanes = 2 * (width // HEADS)
        chunks = width // parts // lanes
        vmem = pltpu.VMEM
        dma = pltpu.SemaphoreType.DMA
        bulk = toks // TILE * TILE
        tail = (2 * views * (toks - bulk) + 7) // 8 * 8
        source = vmem((parts, views, toks, width // parts), BF16)
        packed = vmem((2, chunks, parts, 2 * views * bulk + tail, lanes), BF16)
        edge = vmem((chunks, 2, 2, parts, toks, lanes), BF16)
        rows = vmem((chunks, views + 2, 2, parts * PAD, lanes), BF16)
        cols = vmem((chunks, views + 2, 2, lanes, parts * PAD), BF16)
        sums = vmem((2, views + 2, parts * PAD, lanes), F32)
        shape = jax.ShapeDtypeStruct(queries.shape, BF16)
        flops = 12 * views * parts * toks * 3 * parts * toks * (width // parts)
        results = pl.pallas_call(
            functools.partial(kernel, groups, parts),
            out_shape=(vmem(queries.shape, BF16),) * 4,
            in_specs=[pl.BlockSpec(memory_space=pl.ANY)] * 4,
            out_specs=[pl.BlockSpec(memory_space=pltpu.VMEM)] * 4,
            scratch_shapes=[
                source, source, source, source, packed, packed, packed, packed,
                vmem((2, parts, tail, lanes), F32), edge, edge, rows, cols, sums, sums,
                dma((parts, 4)), dma((chunks, parts, 2)), dma((chunks, parts, 2)),
                dma((chunks, 2)), dma((chunks, 2)), dma((chunks, 2)), dma((chunks, 2)),
                dma((chunks, parts, 2)), dma((chunks, parts, 2)),
            ],
            cost_estimate=pl.CostEstimate(
                flops=flops, bytes_accessed=16 * views * toks * width, transcendentals=0
            ),
            compiler_params=pltpu.CompilerParams(
                collective_id=0, has_side_effects=True, vmem_limit_bytes=58 * 1024 * 1024
            ),
        )(queries, keys, values, grad_out)
        return pl.pallas_call(
            deliver,
            out_shape=(shape,) * 4,
            in_specs=[pl.BlockSpec(memory_space=pltpu.VMEM)] * 4,
            out_specs=[pl.BlockSpec(memory_space=pl.ANY)] * 4,
            scratch_shapes=[dma((4,))],
            compiler_params=pltpu.CompilerParams(vmem_limit_bytes=48 * 1024 * 1024),
        )(*results)

    spec = P("view", "tok", None)
    return jax.shard_map(
        local, mesh=mesh, in_specs=(spec,) * 4, out_specs=(spec,) * 4, check_vma=False
    )
```
